32 devices in a mesh: groups: 2 (over y), req: 4 (over z), tp: 4 (over x, core).
Axes of the slice: x: 2, y: 2, z: 4, core: 2. Of those that a mesh axis runs over, the one named last changes fastest.
Arguments:
- patches: bfloat16 [512, 1280], P(('groups', 'req'), 'tp'), parts along dimension 0, may hold values from -6 to 6
- patch_counts: int32 [8, 2], P('groups'), parts along dimension 0, may hold values from 4 to 32, as said below
- image_request: int32 [8, 2], P('groups'), parts along dimension 0, may hold values from 0 to 3, as said below
- image_position: int32 [8, 2], P('groups'), parts along dimension 0, may hold values from 0 to 504, as said below
- request_lengths: int32 [8], P('groups'), parts along dimension 0, may hold values from 1 to 512, as said below
- vit_gain: float32 [1280], replicated, may hold values from 0.1 to 1.9
- qkv_weight: bfloat16 [1280, 3, 1280], P('req', None, 'tp'), may hold values from -2 to 2
- proj_weight: bfloat16 [1280, 1280], P('tp', 'req'), may hold values from -0.15625 to 0.15625
- merge_gain: float32 [1280], replicated, may hold values from 0.1 to 1.9
- fc1_weight: bfloat16 [5120, 5120], P('req', 'tp'), may hold values from -0.078125 to 0.078125
- fc2_weight: bfloat16 [5120, 8192], P('tp', 'req'), may hold values from -0.078125 to 0.078125
- text_rows: bfloat16 [4096, 8192], P(('groups', 'req'), 'tp'), parts along dimension 0, may hold values from -6 to 6
- rms_gain: float32 [8192], P('tp'), may hold values from 0.1 to 1.9
- kv_weight: bfloat16 [8192, 2, 1024], P('tp'), may hold values from -0.0625 to 0.0625
- kv_scale: float32 [2, 16], replicated, may hold values from 0.004 to 0.04
Outputs:
- kv_cache: bfloat16 [4096, 2, 1024], P(('groups', 'req', 'tp')), parts along dimension 0
The draws below stay inside these ranges and needn't reach their ends.
There are 2 independent parts, one for each index of `groups`. The reference program is written for one: setup_inputs(seed, part) draws one part's arguments, and reference() takes and returns one part's arrays. A program takes and returns all parts, laid end to end along the dimension named above; an argument that names none is the same for every part. Nothing has to cross between parts.
Inputs may be any that keep to these rules, and one draw needn't show every extreme that they name: `patch_counts`: multiples of 4. The images of block s are those of row s; the largest count is reached in every draw. `image_request`: every block of 512 rows of combined holds the placeholders of exactly 2 whole images, at most 16 placeholder rows, and some block holds exactly 16. `image_position`: placeholders of different images never share a row and never cross a block of 512 rows. `request_lengths`: every placeholder row lies before its request's length; one request fills its whole slot.
All inputs are finite; a program needn't handle non-finite values.
Results may differ from the reference program's by a relative error of at most 0.0052.
Values may be sent and summed in bfloat16 or wider, within the bound.
A program may use at most 128 MiB of HBM per device.

```python
import math
import jax
import jax.numpy as jnp
from jax import lax

VIT_D = 1280
VIT_HEADS = 16
VIT_HD = 80
MERGE_W = 5120
D = 8192
KV_HEADS = 8
HEAD_DIM = 128
KV_W = 1024
QGROUP = 64
IMG_DEV = 2
REQS = 4
PATCH_DEV = 64
T_DEV = 512
MRG_IMG = 8
NPATCH = 256
ROWS = 2048
REQ_LEN = 512
N_REQ = 4


def layout_tables(key):
    subkeys = jax.random.split(key, 6)
    images = N_REQ * IMG_DEV
    placing = jax.random.permutation(subkeys[0], images)
    rotation = jax.random.randint(subkeys[2], (), 0, N_REQ)
    final_row = (N_REQ - 1 - rotation) % N_REQ
    final_slot = final_row * IMG_DEV + IMG_DEV - 1
    merged_sizes = jax.random.randint(subkeys[1], (images,), 1, MRG_IMG + 1)
    merged_sizes = jnp.where((placing < IMG_DEV) | (placing == final_slot), MRG_IMG, merged_sizes)
    slot_sizes = jnp.zeros((images,), jnp.int32).at[placing].set(merged_sizes).reshape(N_REQ, IMG_DEV)
    gap_most = (T_DEV - IMG_DEV * MRG_IMG) // IMG_DEV
    gap_rows = jax.random.randint(subkeys[3], (N_REQ, IMG_DEV), 0, gap_most + 1)
    earlier = jnp.sum((gap_rows + slot_sizes)[:, :IMG_DEV - 1], axis=1)
    last_gap = T_DEV - MRG_IMG - earlier
    row_ids = jnp.arange(N_REQ, dtype=jnp.int32)
    column_ids = jnp.arange(IMG_DEV, dtype=jnp.int32)
    forced = (row_ids[:, None] == final_row) & (column_ids[None, :] == IMG_DEV - 1)
    gap_rows = jnp.where(forced, last_gap[:, None], gap_rows)
    span_ends = jnp.cumsum(gap_rows + slot_sizes, axis=1)
    starts = span_ends - slot_sizes
    owners = (row_ids + rotation) % N_REQ
    global_start = (owners[:, None] * T_DEV + starts).reshape(-1)
    global_end = (owners[:, None] * T_DEV + span_ends).reshape(-1)
    slot_request = global_start // REQ_LEN
    request_ids = jnp.arange(REQS, dtype=jnp.int32)
    last_end = jnp.max(jnp.where(slot_request[None, :] == request_ids[:, None], global_end[None, :] - request_ids[:, None] * REQ_LEN, 0), axis=1)
    shortened = REQ_LEN - jax.random.randint(subkeys[4], (REQS,), 0, T_DEV)
    lengths = jnp.maximum(shortened, last_end)
    longest = jax.random.randint(subkeys[5], (), 0, REQS)
    lengths = jnp.where(request_ids == longest, REQ_LEN, lengths).astype(jnp.int32)
    counts = (4 * merged_sizes).reshape(N_REQ, IMG_DEV).astype(jnp.int32)
    image_req = slot_request[placing].reshape(N_REQ, IMG_DEV).astype(jnp.int32)
    image_pos = (global_start % REQ_LEN)[placing].reshape(N_REQ, IMG_DEV).astype(jnp.int32)
    return (counts, image_req, image_pos, lengths)


def draw_patch_counts(key, part):
    return layout_tables(key)[0]


def draw_image_request(key, part):
    return layout_tables(key)[1]


def draw_image_position(key, part):
    return layout_tables(key)[2]


def draw_request_lengths(key, part):
    return layout_tables(key)[3]


def draw_qkv_weight(key, part):
    key = jax.random.fold_in(key, 7)
    noise_key = jax.random.fold_in(key, 0)
    drawn = jax.random.normal(noise_key, (VIT_D, 3, VIT_D), jnp.float32) * VIT_D ** (-0.5)
    return jnp.clip(drawn, -2.0, 2.0).astype(jnp.bfloat16)


def shard_levels(rng, extent, cuts, low, top_value):
    def one(dim, blocks):
        draws = jax.random.uniform(jax.random.fold_in(jax.random.fold_in(rng, 6), dim), (blocks,), jnp.float32, low / len(cuts), top_value / len(cuts))
        return jnp.repeat(jnp.exp(draws), extent[dim] // blocks).reshape((-1,) + (1,) * (len(extent) - dim - 1))

    level = one(*cuts[0])
    for cut in cuts[1:]:
        level = level * one(*cut)
    return level


def scatter_about(key, extent, scale, limit, shards=(), held_as=jnp.bfloat16):
    entries = scale * jax.random.normal(key, extent, jnp.float32)
    if shards:
        entries = entries * shard_levels(key, extent, shards, -0.22, 0.18)
    return jnp.clip(entries, -limit, limit).astype(held_as)


def setup_inputs(seed: int = 0, part: int = 0) -> dict:
    seeds = jax.random.split(jax.random.key(seed), 16)
    part_splits = jax.random.split(jax.random.fold_in(seeds[15], part), 16)
    return {
        "patches": scatter_about(part_splits[0], (NPATCH, VIT_D), 1.0, 6.0, ((0, 4), (1, 4))),
        "patch_counts": draw_patch_counts(jax.random.fold_in(jax.random.fold_in(seeds[15], part), 71), part),
        "image_request": draw_image_request(jax.random.fold_in(jax.random.fold_in(seeds[15], part), 71), part),
        "image_position": draw_image_position(jax.random.fold_in(jax.random.fold_in(seeds[15], part), 71), part),
        "request_lengths": draw_request_lengths(jax.random.fold_in(jax.random.fold_in(seeds[15], part), 71), part),
        "vit_gain": jnp.clip(1.0 + 0.18 * jax.random.normal(seeds[5], (VIT_D,), jnp.float32), 0.1, 1.9),
        "qkv_weight": draw_qkv_weight(jax.random.fold_in(seeds[15], 71), part),
        "proj_weight": scatter_about(seeds[7], (VIT_D, VIT_D), VIT_D ** -0.5, 0.15625, ((0, 4), (1, 4))),
        "merge_gain": jnp.clip(1.0 + 0.18 * jax.random.normal(seeds[8], (VIT_D,), jnp.float32), 0.1, 1.9),
        "fc1_weight": scatter_about(seeds[9], (MERGE_W, MERGE_W), MERGE_W ** -0.5, 0.078125, ((0, 4), (1, 4))),
        "fc2_weight": scatter_about(seeds[10], (MERGE_W, D), MERGE_W ** -0.5, 0.078125, ((0, 4), (1, 4))),
        "text_rows": scatter_about(part_splits[11], (ROWS, D), 1.0, 6.0, ((0, 4), (1, 4))),
        "rms_gain": jnp.clip(1.0 + 0.18 * jax.random.normal(seeds[12], (D,), jnp.float32), 0.1, 1.9),
        "kv_weight": scatter_about(seeds[13], (D, 2, KV_W), D ** -0.5, 0.0625, ((0, 4),)),
        "kv_scale": jnp.clip(jnp.exp(jax.random.uniform(seeds[14], (2, KV_W // QGROUP), jnp.float32, math.log(0.004), math.log(0.04))), 0.004, 0.04),
    }


epsilon = 1e-06
theta_base = 1000000.0
clip_level = 127.0

def layer_norm(values, gains):
    average = lax.optimization_barrier(jnp.mean(values, axis=-1, keepdims=True))
    centred = values - average
    variance = lax.optimization_barrier(jnp.mean(centred * centred, axis=-1, keepdims=True))
    return centred * lax.rsqrt(variance + epsilon) * gains

def patch_images(counts_row, patch_rows):
    bounds = jnp.cumsum(counts_row)
    row_ids = jnp.arange(patch_rows, dtype=jnp.int32)
    return lax.optimization_barrier(jnp.sum((row_ids[:, None] >= bounds[None, :]).astype(jnp.int32), axis=1))

def attend_wide(queries, keys_in, values_in, image_ids, factor):
    scores = jnp.einsum('qhd,khd->hqk', queries, keys_in) * factor
    allowed = image_ids[:, None] == image_ids[None, :]
    scores = jnp.where(allowed[None], scores, -jnp.inf)
    weights = jax.nn.softmax(scores, axis=-1).astype(jnp.bfloat16)
    return jnp.einsum('hqk,khd->qhd', weights.astype(jnp.float32), values_in).astype(jnp.bfloat16)

def visual_targets(patch_counts, image_request, image_position, merged_dev, request_len):
    merged_runs = patch_counts // 4
    run_ends = jnp.cumsum(merged_runs, axis=1)
    run_starts = run_ends - merged_runs
    row_ids = jnp.arange(merged_dev, dtype=jnp.int32)
    inside = (row_ids[None, :, None] >= run_starts[:, None, :]) & (row_ids[None, :, None] < run_ends[:, None, :])
    offsets = image_request * request_len + image_position - run_starts
    target = lax.optimization_barrier(jnp.sum(jnp.where(inside, offsets[:, None, :] + row_ids[None, :, None], 0), axis=2))
    is_live = jnp.any(inside, axis=2)
    return (target.reshape(-1).astype(jnp.int32), is_live.reshape(-1))

def rotate_keys(heads, positions):
    half_dim = heads.shape[-1] // 2
    frequency = theta_base ** (-2.0 * jnp.arange(half_dim, dtype=jnp.float32) / heads.shape[-1])
    angles = positions.astype(jnp.float32)[:, None] * frequency[None, :]
    cosine = jnp.cos(angles)[:, None, :]
    sine = jnp.sin(angles)[:, None, :]
    former = heads[..., :half_dim]
    latter = heads[..., half_dim:]
    return jnp.concatenate([former * cosine - latter * sine, latter * cosine + former * sine], axis=-1)

def finish_cache(stacked, positions, live_rows, kv_scale):
    height = stacked.shape[0]
    rotated = rotate_keys(stacked[:, 0].reshape(height, KV_HEADS, HEAD_DIM), positions)
    joined = jnp.concatenate([rotated.reshape(height, 1, KV_HEADS * HEAD_DIM), stacked[:, 1:2]], axis=1)
    bounds = jnp.repeat(clip_level * kv_scale, QGROUP, axis=1)
    clipped = jnp.clip(joined, -bounds, bounds)
    return jnp.where(live_rows[:, None, None], clipped, 0.0).astype(jnp.bfloat16)

def reference(patches, patch_counts, image_request, image_position, request_lengths, vit_gain, qkv_weight, proj_weight, merge_gain, fc1_weight, fc2_weight, text_rows, rms_gain, kv_weight, kv_scale):
    qkv_wide = qkv_weight.astype(jnp.float32)

    def vision_block(pair):
        block_rows, counts_row = pair
        image_ids = patch_images(counts_row, PATCH_DEV)
        normed = layer_norm(block_rows.astype(jnp.float32), vit_gain).astype(jnp.bfloat16)
        qkv_all = jnp.einsum('pd,dcf->pcf', normed.astype(jnp.float32), qkv_wide).astype(jnp.bfloat16)
        heads = qkv_all.reshape(PATCH_DEV, 3, VIT_HEADS, VIT_HD).astype(jnp.float32)
        attended = attend_wide(heads[:, 0], heads[:, 1], heads[:, 2], image_ids, VIT_HD ** (-0.5))
        branch = jnp.dot(attended.reshape(PATCH_DEV, VIT_D), proj_weight, preferred_element_type=jnp.float32)
        hidden = (block_rows.astype(jnp.float32) + branch).astype(jnp.bfloat16)
        normed_out = layer_norm(hidden.astype(jnp.float32), merge_gain).astype(jnp.bfloat16)
        return normed_out.reshape(PATCH_DEV // 4, MERGE_W)
    merged_all = lax.map(vision_block, (patches.reshape(N_REQ, PATCH_DEV, VIT_D), patch_counts))
    merged_all = merged_all.reshape(N_REQ * (PATCH_DEV // 4), MERGE_W)
    activated = jax.nn.gelu(jnp.dot(merged_all, fc1_weight, preferred_element_type=jnp.float32), approximate=False).astype(jnp.bfloat16)
    visual = jnp.dot(activated, fc2_weight, preferred_element_type=jnp.float32).astype(jnp.bfloat16)
    target, is_live = visual_targets(patch_counts, image_request, image_position, PATCH_DEV // 4, REQ_LEN)
    combined = text_rows.at[jnp.where(is_live, target, ROWS)].set(visual, mode='drop')
    kv_wide = kv_weight.astype(jnp.float32)

    def cache_block(pair):
        block_rows, block_index = pair
        wide = block_rows.astype(jnp.float32)
        scaled = (wide * lax.rsqrt(lax.optimization_barrier(jnp.mean(wide * wide, axis=1, keepdims=True)) + epsilon) * rms_gain).astype(jnp.bfloat16)
        stacked = jnp.einsum('rf,fcw->rcw', scaled.astype(jnp.float32), kv_wide)
        row_ids = block_index * T_DEV + jnp.arange(T_DEV, dtype=jnp.int32)
        positions = row_ids % REQ_LEN
        live_rows = positions < request_lengths[row_ids // REQ_LEN]
        return finish_cache(stacked, positions, live_rows, kv_scale)
    caches = lax.map(cache_block, (combined.reshape(N_REQ, T_DEV, D), jnp.arange(N_REQ, dtype=jnp.int32)))
    return caches.reshape(ROWS, 2, KV_HEADS * HEAD_DIM)
```

```python
import functools

import jax
import jax.numpy as jnp
from jax import lax
from jax.experimental import pallas as pl
from jax.experimental.pallas import tpu as pltpu
from jax.sharding import PartitionSpec as P

VIT_HEADS = 16
VIT_HD = 80
D = 8192
KV_HEADS = 8
HEAD_DIM = 128
QGROUP = 64


epsilon = 1e-06
theta_base = 1000000.0
clip_level = 127.0


def layer_norm(values, gains):
    average = jnp.mean(values, axis=-1, keepdims=True)
    centred = values - average
    variance = jnp.mean(centred * centred, axis=-1, keepdims=True)
    return centred * lax.rsqrt(variance + epsilon) * gains


def patch_images(counts_row, patch_rows):
    bounds = jnp.cumsum(counts_row)
    row_ids = jnp.arange(patch_rows, dtype=jnp.int32)
    return jnp.sum((row_ids[:, None] >= bounds[None, :]).astype(jnp.int32), axis=1)


def attend(queries, keys_in, values_in, image_ids, factor):
    scores = (
        jnp.einsum("qhd,khd->hqk", queries, keys_in, preferred_element_type=jnp.float32) * factor
    )
    allowed = image_ids[:, None] == image_ids[None, :]
    scores = jnp.where(allowed[None], scores, -jnp.inf)
    weights = jax.nn.softmax(scores, axis=-1).astype(jnp.bfloat16)
    return jnp.einsum(
        "hqk,khd->qhd", weights, values_in, preferred_element_type=jnp.float32
    ).astype(jnp.bfloat16)


def visual_targets(patch_counts, image_request, image_position, merged_dev, request_len):
    merged_runs = patch_counts // 4
    run_ends = jnp.cumsum(merged_runs, axis=1)
    run_starts = run_ends - merged_runs
    row_ids = jnp.arange(merged_dev, dtype=jnp.int32)
    inside = (row_ids[None, :, None] >= run_starts[:, None, :]) & (
        row_ids[None, :, None] < run_ends[:, None, :]
    )
    offsets = image_request * request_len + image_position - run_starts
    target = jnp.sum(jnp.where(inside, offsets[:, None, :] + row_ids[None, :, None], 0), axis=2)
    is_live = jnp.any(inside, axis=2)
    return (target.reshape(-1), is_live.reshape(-1))


def rotate_keys(heads, positions):
    half_dim = heads.shape[-1] // 2
    frequency = theta_base ** (-2.0 * jnp.arange(half_dim, dtype=jnp.float32) / heads.shape[-1])
    angles = positions.astype(jnp.float32)[:, None] * frequency[None, :]
    cosine = jnp.cos(angles)[:, None, :]
    sine = jnp.sin(angles)[:, None, :]
    former = heads[..., :half_dim]
    latter = heads[..., half_dim:]
    return jnp.concatenate(
        [former * cosine - latter * sine, latter * cosine + former * sine], axis=-1
    )


def finish_cache(stacked, positions, live_rows, kv_scale):
    height = stacked.shape[0]
    rotated = rotate_keys(stacked[:, 0].reshape(height, KV_HEADS, HEAD_DIM), positions)
    joined = jnp.concatenate(
        [rotated.reshape(height, 1, KV_HEADS * HEAD_DIM), stacked[:, 1:2]], axis=1
    )
    bounds = jnp.repeat(clip_level * kv_scale, QGROUP, axis=1)
    clipped = jnp.clip(joined, -bounds, bounds)
    return jnp.where(live_rows[:, None, None], clipped, 0.0).astype(jnp.bfloat16)


def general_body(
    patches,
    patch_counts,
    image_request,
    image_position,
    request_lengths,
    vit_gain,
    qkv_weight,
    proj_weight,
    merge_gain,
    fc1_weight,
    fc2_weight,
    text_rows,
    rms_gain,
    kv_weight,
    kv_scale,
):
    req_devices = lax.axis_size("req")
    tp_devices = lax.axis_size("tp")
    req_index = lax.axis_index("req")
    tp_index = lax.axis_index("tp")
    patch_rows = patches.shape[0]
    merged_rows = patch_rows // 4
    token_rows = text_rows.shape[0]
    request_len = req_devices * token_rows // request_lengths.shape[0]
    local_heads = VIT_HEADS // tp_devices
    gathered = lax.all_gather(patches, "tp", axis=1, tiled=True)
    vit_width = gathered.shape[1]
    normed = layer_norm(gathered.astype(jnp.float32), vit_gain).astype(jnp.bfloat16)
    qkv_local = jnp.einsum(
        "pd,dcf->pcf",
        normed,
        lax.all_gather(qkv_weight, "req", axis=0, tiled=True),
        preferred_element_type=jnp.float32,
    ).astype(jnp.bfloat16)
    heads = qkv_local.reshape(patch_rows, 3, local_heads, VIT_HD)
    image_ids = patch_images(patch_counts[req_index], patch_rows)
    attended = attend(heads[:, 0], heads[:, 1], heads[:, 2], image_ids, VIT_HD ** (-0.5))
    flat_heads = attended.reshape(patch_rows, local_heads * VIT_HD)
    branch = jnp.dot(
        flat_heads,
        lax.all_gather(proj_weight, "req", axis=1, tiled=True),
        preferred_element_type=jnp.float32,
    )
    branch_total = lax.psum(branch, "tp")
    hidden = (gathered.astype(jnp.float32) + branch_total).astype(jnp.bfloat16)
    merged_norm = layer_norm(hidden.astype(jnp.float32), merge_gain).astype(jnp.bfloat16)
    merged = merged_norm.reshape(merged_rows, 4 * vit_width)
    feature_blocks = lax.all_to_all(merged, "req", split_axis=1, concat_axis=0, tiled=True)
    picked = feature_blocks
    before_gelu = lax.psum_scatter(
        jnp.dot(picked, fc1_weight, preferred_element_type=jnp.float32),
        "req",
        scatter_dimension=0,
        tiled=True,
    )
    activated = jax.nn.gelu(before_gelu, approximate=False).astype(jnp.bfloat16)
    outward = jnp.dot(
        lax.all_gather(activated, "req", axis=0, tiled=True),
        fc2_weight,
        preferred_element_type=jnp.float32,
    )
    target, is_live = visual_targets(
        patch_counts, image_request, image_position, merged_rows, request_len
    )
    all_rows = req_devices * token_rows
    slot_total = req_devices * merged_rows
    source_total = outward.shape[0]
    flags = (
        jnp.zeros((all_rows,), jnp.int32)
        .at[jnp.where(is_live, target, all_rows)]
        .set(1, mode="drop")
    )
    flag_grid = flags.reshape(req_devices, token_rows)
    ranks = (jnp.cumsum(flag_grid, axis=1) - flag_grid).reshape(-1)
    owners = target // token_rows
    slots = owners * merged_rows + ranks[jnp.clip(target, 0, all_rows - 1)]
    source_ids = jnp.arange(source_total, dtype=jnp.int32)
    picking = (
        jnp.full((slot_total,), source_total, jnp.int32)
        .at[jnp.where(is_live, slots, slot_total)]
        .set(source_ids, mode="drop")
    )
    padded = jnp.concatenate([outward, jnp.zeros((1, outward.shape[1]), jnp.float32)], axis=0)
    sending = padded[picking]
    arrived = lax.all_to_all(sending, "req", split_axis=0, concat_axis=1, tiled=True)
    visual = lax.psum_scatter(arrived, "tp", scatter_dimension=1, tiled=True).astype(jnp.bfloat16)
    local_flags = lax.dynamic_slice_in_dim(flags, req_index * token_rows, token_rows)
    local_ranks = lax.dynamic_slice_in_dim(ranks, req_index * token_rows, token_rows)
    chosen = visual[jnp.clip(local_ranks, 0, merged_rows - 1)]
    combined = jnp.where(local_flags[:, None] > 0, chosen, text_rows)
    wide_rows = combined.astype(jnp.float32)
    square_sums = lax.psum(jnp.sum(wide_rows * wide_rows, axis=1), "tp")
    scaled = (wide_rows * lax.rsqrt(square_sums[:, None] / D + epsilon) * rms_gain).astype(
        jnp.bfloat16
    )
    share_rows = token_rows // tp_devices
    picked = scaled
    stacked = lax.psum_scatter(
        jnp.einsum("rf,fcw->rcw", picked, kv_weight, preferred_element_type=jnp.float32),
        "tp",
        scatter_dimension=0,
        tiled=True,
    )
    row_ids = (
        req_index * token_rows + tp_index * share_rows + jnp.arange(share_rows, dtype=jnp.int32)
    )
    positions = row_ids % request_len
    live_rows = positions < request_lengths[row_ids // request_len]
    return finish_cache(stacked, positions, live_rows, kv_scale)


def iota(shape, dim):
    return lax.broadcasted_iota(jnp.int32, shape, dim)


def f32_dot(left, right):
    return jnp.dot(left, right, preferred_element_type=jnp.float32)


def image_table(counts, image_request, image_position, request_len, token_rows):
    images = []
    for s in range(counts.shape[0]):
        source = jnp.int32(s * SLOTS)
        for j in range(counts.shape[1]):
            run = counts[s, j] // 4
            first = image_request[s, j] * request_len + image_position[s, j]
            images.append((source, first, run, first // token_rows))
            source = source + run
    table = []
    for source, first, run, owner in images:
        base = jnp.int32(0)
        for _, other_first, other_run, other_owner in images:
            earlier = (other_owner == owner) & (other_first < first)
            base = base + jnp.where(earlier, other_run, 0)
        table.append((source, first, run, owner, base))
    return table


SLOTS = 16
SIDE = 4


def vision_kernel(
    request_len,
    token_rows,
    counts,
    image_request,
    image_position,
    patches,
    vit_gain,
    merge_gain,
    rms_gain,
    qkv_hbm,
    proj_hbm,
    fc1_hbm,
    fc2_hbm,
    kv_hbm,
    placed_ref,
    qkv_w,
    proj_w,
    fc1_w,
    fc2_w,
    kv_w,
    load_sem,
    patch_all,
    res_out,
    res_in,
    norm_out,
    norm_in,
    part_own,
    part_out,
    part_in,
    att_out,
    att_in,
    branch_out,
    branch_in,
    hid_out,
    hid_in,
    pre_own,
    pre_out,
    pre_in,
    act_out,
    act_in,
    vis_out,
    vis_in,
    row_out,
    row_in,
    sq_out,
    sq_in,
    send_sem,
    recv_sem,
):
    r = lax.axis_index("req")
    t = lax.axis_index("tp")
    rows, width = patches.shape
    full = SIDE * width

    def other(i, d):
        return lax.rem(i + d, SIDE)

    loads = []
    for k, (src, dst) in enumerate(
        ((qkv_hbm, qkv_w), (proj_hbm, proj_w), (fc1_hbm, fc1_w), (fc2_hbm, fc2_w), (kv_hbm, kv_w))
    ):
        copy = pltpu.make_async_copy(src, dst, load_sem.at[k])
        copy.start()
        loads.append(copy)

    barrier = pltpu.get_barrier_semaphore()
    for a in range(SIDE):
        for b in range(SIDE):
            if a or b:
                pl.semaphore_signal(
                    barrier,
                    inc=1,
                    device_id={"req": other(r, a), "tp": other(t, b)},
                    device_id_type=pl.DeviceIdType.MESH,
                )
    pl.semaphore_wait(barrier, SIDE * SIDE - 1)

    pending = []

    def remote(src, dst, stage, s_index, r_index, to_r, to_t):
        return pltpu.make_async_remote_copy(
            src_ref=src,
            dst_ref=dst,
            send_sem=send_sem.at[stage, s_index],
            recv_sem=recv_sem.at[stage, r_index],
            device_id={"req": to_r, "tp": to_t},
            device_id_type=pl.DeviceIdType.MESH,
        )

    def send(copy, unless=None):
        if unless is None:
            copy.start()
            pending.append(copy.wait_send)
        else:
            pl.when(jnp.logical_not(unless))(copy.start)
            pending.append(lambda: pl.when(jnp.logical_not(unless))(copy.wait_send))

    def receive(dst, stage, index, unless=None):
        copy = remote(dst, dst, stage, 0, index, other(r, 1), t)
        if unless is None:
            copy.wait_recv()
        else:
            pl.when(jnp.logical_not(unless))(copy.wait_recv)

    on_diagonal = r == t

    for d in range(1, SIDE):
        send(remote(patches, patch_all.at[t], 0, d, d, r, other(t, d)))
    patch_all[t] = patches[...]
    picks_i = iota((rows, rows), 0)
    picks_j = iota((rows, rows), 1)
    by_class = jnp.where(
        picks_j == 4 * lax.rem(picks_i, SLOTS) + picks_i // SLOTS, 1.0, 0.0
    ).astype(jnp.bfloat16)
    regrouped = f32_dot(by_class, patches[...]).astype(jnp.bfloat16)
    for c in range(SIDE):
        res_out[c] = regrouped[c * SLOTS : (c + 1) * SLOTS]
    for d in range(SIDE):
        c = other(t, d)
        unless = on_diagonal if d == 0 else None
        send(remote(res_out.at[c], res_in.at[r], 1, d, r, t, c), unless)

    @pl.when(on_diagonal)
    def _():
        res_in[r] = res_out[t]

    for d in range(1, SIDE):
        receive(patch_all.at[other(t, SIDE - d)], 0, d)

    def chunk_norm(values, gains):
        total = jnp.sum(values[0], axis=1, keepdims=True)
        for v in values[1:]:
            total = total + jnp.sum(v, axis=1, keepdims=True)
        average = total / full
        centred = [v - average for v in values]
        total = jnp.sum(centred[0] * centred[0], axis=1, keepdims=True)
        for v in centred[1:]:
            total = total + jnp.sum(v * v, axis=1, keepdims=True)
        inverse = lax.rsqrt(total / full + epsilon)
        return [
            (v * inverse * gains[c : c + 1, :]).astype(jnp.bfloat16)
            for c, v in enumerate(centred)
        ]

    normed = chunk_norm([patch_all[c].astype(jnp.float32) for c in range(SIDE)], vit_gain)
    for c in range(SIDE):
        norm_out[c] = normed[c]
    for d in range(1, SIDE):
        p = other(r, d)
        send(remote(norm_out.at[p], norm_in.at[r], 2, d, d, p, t))
    norm_in[r] = norm_out[r]
    for d in range(1, SIDE):
        receive(norm_in.at[other(r, SIDE - d)], 2, d)

    loads[0].wait()
    every = norm_in[...].reshape(SIDE * rows, width)
    for c in range(3):
        part = f32_dot(every, qkv_w[c]).reshape(SIDE, rows, width)
        part_own[:, c] = part
        part_out[:, c] = part.astype(jnp.bfloat16)
    for d in range(1, SIDE):
        p = other(r, d)
        send(remote(part_out.at[p], part_in.at[d - 1], 3, d, d, p, t))
    total = part_own[r]
    for d in range(1, SIDE):
        receive(part_in.at[d - 1], 3, d)
        total = total + part_in[d - 1].astype(jnp.float32)
    qkv = total.astype(jnp.bfloat16)

    first_end = counts[r, 0]
    second_end = first_end + counts[r, 1]

    def ids(index):
        return (index >= first_end).astype(jnp.int32) + (index >= second_end).astype(jnp.int32)

    allowed = ids(picks_i) == ids(picks_j)
    lanes = iota((rows, width), 1) // VIT_HD
    attended = jnp.zeros((rows, width), jnp.float32)
    for h in range(width // VIT_HD):
        mine = lanes == h
        query = jnp.where(mine, qkv[0].astype(jnp.float32), 0.0).astype(jnp.bfloat16)
        value = jnp.where(mine, qkv[2].astype(jnp.float32), 0.0).astype(jnp.bfloat16)
        scores = lax.dot_general(
            query, qkv[1], (((1,), (1,)), ((), ())), preferred_element_type=jnp.float32
        ) * (VIT_HD ** (-0.5))
        scores = jnp.where(allowed, scores, -jnp.inf)
        weights = jnp.exp(scores - jnp.max(scores, axis=1, keepdims=True))
        weights = weights / jnp.sum(weights, axis=1, keepdims=True)
        attended = attended + f32_dot(weights.astype(jnp.bfloat16), value)
    att_out[...] = f32_dot(by_class, attended.astype(jnp.bfloat16)).astype(jnp.bfloat16)
    for d in range(1, SIDE):
        send(remote(att_out, att_in.at[r], 4, d, d, other(r, d), t))
    att_in[r] = att_out[...]
    loads[1].wait()
    for d in range(1, SIDE):
        receive(att_in.at[other(r, SIDE - d)], 4, d)

    branch = f32_dot(att_in[...].reshape(SIDE * rows, width), proj_w[...])
    branch = branch.reshape(SIDE, SIDE, SLOTS, width)
    for c in range(SIDE):
        branch_out[c] = branch[:, c].reshape(rows, width)
    for d in range(1, SIDE):
        c = other(t, d)
        send(remote(branch_out.at[c], branch_in.at[d - 1], 5, d, d, r, c))
    total = branch_out[t]
    for d in range(SIDE):
        q = other(r, d)
        receive(res_in.at[q], 1, q, on_diagonal if d == 0 else None)
    residual = res_in[...].reshape(rows, width).astype(jnp.float32)
    for d in range(1, SIDE):
        receive(branch_in.at[d - 1], 5, d)
        total = total + branch_in[d - 1]
    hid_out[...] = (residual + total).astype(jnp.bfloat16)
    for d in range(SIDE):
        unless = on_diagonal if d == 0 else None
        send(remote(hid_out, hid_in.at[r], 6, d, r, t, other(t, d)), unless)

    @pl.when(on_diagonal)
    def _():
        hid_in[r] = hid_out[...]

    loads[2].wait()
    for d in range(SIDE):
        q = other(r, d)
        receive(hid_in.at[q], 6, q, on_diagonal if d == 0 else None)

    merged = chunk_norm([hid_in[c].astype(jnp.float32) for c in range(SIDE)], merge_gain)
    before = f32_dot(merged[0], fc1_w[0:width])
    for c in range(1, SIDE):
        before = before + f32_dot(merged[c], fc1_w[c * width : (c + 1) * width])
    for q in range(SIDE):
        pre_own[q] = before[q * SLOTS : (q + 1) * SLOTS]
        pre_out[q] = before[q * SLOTS : (q + 1) * SLOTS].astype(jnp.bfloat16)
    for d in range(1, SIDE):
        p = other(r, d)
        send(remote(pre_out.at[p], pre_in.at[d - 1], 7, d, d, p, t))
    total = pre_own[r]
    for d in range(1, SIDE):
        receive(pre_in.at[d - 1], 7, d)
        total = total + pre_in[d - 1].astype(jnp.float32)
    act_out[...] = (0.5 * total * (1.0 + lax.erf(total * (0.5**0.5)))).astype(jnp.bfloat16)
    for d in range(1, SIDE):
        send(remote(act_out, act_in.at[r], 8, d, d, other(r, d), t))
    act_in[r] = act_out[...]
    table = image_table(counts, image_request, image_position, request_len, token_rows)
    slot_i = iota((SIDE * SLOTS, SIDE * SLOTS), 0)
    row_j = iota((SIDE * SLOTS, SIDE * SLOTS), 1)
    pick = jnp.zeros(slot_i.shape, jnp.float32)
    for source, _, run, owner, base in table:
        offset = row_j - source
        hit = (slot_i - (owner * SLOTS + base) == offset) & (offset >= 0) & (offset < run)
        pick = jnp.where(hit, 1.0, pick)
    pick = pick.astype(jnp.bfloat16)
    loads[3].wait()
    for d in range(1, SIDE):
        receive(act_in.at[other(r, SIDE - d)], 8, d)

    active = act_in[...].reshape(SIDE * SLOTS, act_in.shape[2])
    picked = f32_dot(pick, active).astype(jnp.bfloat16)
    outward = f32_dot(picked, fc2_w[...]).astype(jnp.bfloat16)
    for q in range(SIDE):
        vis_out[q] = outward[q * SLOTS : (q + 1) * SLOTS]
    for d in range(SIDE):
        q = other(r, d)
        unless = on_diagonal if d == 0 else None
        send(remote(vis_out.at[q], vis_in.at[t], 9, d, t, q, r), unless)

    @pl.when(on_diagonal)
    def _():
        vis_in[t] = vis_out[r]

    loads[4].wait()
    for d in range(SIDE):
        q = other(t, d)
        receive(vis_in.at[q], 9, q, on_diagonal if d == 0 else None)
    visual = vis_in[0].astype(jnp.float32)
    for q in range(1, SIDE):
        visual = visual + vis_in[q].astype(jnp.float32)
    visual = visual.astype(jnp.bfloat16).astype(jnp.float32)
    squares = jnp.sum(visual * visual, axis=1, keepdims=True)
    sq_out[...] = jnp.broadcast_to(squares, sq_out.shape)
    for d in range(1, SIDE):
        send(remote(sq_out, sq_in.at[d - 1], 10, d, d, r, other(t, d)))
    projected = f32_dot((visual * rms_gain[...]).astype(jnp.bfloat16), kv_w[...])
    row_out[...] = projected.astype(jnp.bfloat16)
    for d in range(1, SIDE):
        send(remote(row_out, row_in.at[d - 1], 11, d, d, r, other(t, d)))
    total = projected
    squares = sq_out[...]
    for d in range(1, SIDE):
        receive(sq_in.at[d - 1], 10, d)
        squares = squares + sq_in[d - 1]
        receive(row_in.at[d - 1], 11, d)
        total = total + row_in[d - 1].astype(jnp.float32)
    total = total * lax.rsqrt(squares[:, :1] / (SIDE * visual.shape[1]) + epsilon)
    share = placed_ref.shape[0]
    place_i = iota((share, SLOTS), 0) + r * token_rows + t * share
    place_k = iota((share, SLOTS), 1)
    place = jnp.zeros((share, SLOTS), jnp.float32)
    for _, first, run, owner, base in table:
        offset = place_i - first
        hit = (owner == r) & (place_k - base == offset) & (offset >= 0) & (offset < run)
        place = jnp.where(hit, 1.0, place)
    placed_ref[...] = jnp.dot(
        place, total, preferred_element_type=jnp.float32, precision=lax.Precision.HIGHEST
    )
    for wait in pending:
        wait()


def vision_rows(
    request_len,
    token_rows,
    patch_counts,
    image_request,
    image_position,
    patches,
    vit_gain,
    merge_gain,
    rms_gain,
    qkv_weight,
    proj_weight,
    fc1_weight,
    fc2_weight,
    kv_flat,
):
    rows, width = patches.shape
    hidden_w = fc1_weight.shape[1]
    share_w, kv_width = kv_flat.shape
    bf16, f32 = jnp.bfloat16, jnp.float32
    n = SIDE
    smem = pl.BlockSpec(memory_space=pltpu.SMEM)
    vmem = pl.BlockSpec(memory_space=pltpu.VMEM)
    anywhere = pl.BlockSpec(memory_space=pl.ANY)
    buffers = [
        ((3, width, width), bf16),
        (proj_weight.shape, bf16),
        (fc1_weight.shape, bf16),
        (fc2_weight.shape, bf16),
        (kv_flat.shape, bf16),
        None,
        ((n, rows, width), bf16),
        ((n, SLOTS, width), bf16),
        ((n, SLOTS, width), bf16),
        ((n, rows, width), bf16),
        ((n, rows, width), bf16),
        ((n, 3, rows, width), f32),
        ((n, 3, rows, width), bf16),
        ((n - 1, 3, rows, width), bf16),
        ((rows, width), bf16),
        ((n, rows, width), bf16),
        ((n, rows, width), f32),
        ((n - 1, rows, width), f32),
        ((rows, width), bf16),
        ((n, rows, width), bf16),
        ((n, SLOTS, hidden_w), f32),
        ((n, SLOTS, hidden_w), bf16),
        ((n - 1, SLOTS, hidden_w), bf16),
        ((SLOTS, hidden_w), bf16),
        ((n, SLOTS, hidden_w), bf16),
        ((n, SLOTS, share_w), bf16),
        ((n, SLOTS, share_w), bf16),
        ((SLOTS, kv_width), bf16),
        ((n - 1, SLOTS, kv_width), bf16),
        ((SLOTS, 128), f32),
        ((n - 1, SLOTS, 128), f32),
    ]
    scratch = [
        pltpu.SemaphoreType.DMA((5,)) if b is None else pltpu.VMEM(*b) for b in buffers
    ] + [pltpu.SemaphoreType.DMA((12, n)), pltpu.SemaphoreType.DMA((12, n))]
    return pl.pallas_call(
        functools.partial(vision_kernel, request_len, token_rows),
        out_shape=jax.ShapeDtypeStruct((token_rows // n, kv_width), f32),
        in_specs=[smem] * 3 + [vmem] * 4 + [anywhere] * 5,
        out_specs=vmem,
        scratch_shapes=scratch,
        compiler_params=pltpu.CompilerParams(
            collective_id=0, has_side_effects=True, vmem_limit_bytes=48 * 1024 * 1024
        ),
        cost_estimate=pl.CostEstimate(
            flops=2 * 10**9, bytes_accessed=20 * 10**6, transcendentals=10**5
        ),
    )(
        patch_counts,
        image_request,
        image_position,
        patches,
        vit_gain.reshape(n, width),
        merge_gain.reshape(n, width),
        rms_gain.reshape(1, share_w),
        jnp.transpose(qkv_weight, (1, 0, 2)),
        proj_weight,
        fc1_weight,
        fc2_weight,
        kv_flat,
    )


def square_body(
    patches,
    patch_counts,
    image_request,
    image_position,
    request_lengths,
    vit_gain,
    qkv_weight,
    proj_weight,
    merge_gain,
    fc1_weight,
    fc2_weight,
    text_rows,
    rms_gain,
    kv_weight,
    kv_scale,
):
    req_index = lax.axis_index("req")
    tp_index = lax.axis_index("tp")
    token_rows, share_w = text_rows.shape
    request_len = SIDE * token_rows // request_lengths.shape[0]
    share_rows = token_rows // SIDE
    kv_flat = kv_weight.reshape(share_w, -1)
    wide = text_rows.astype(jnp.float32)
    part = f32_dot((wide * rms_gain).astype(jnp.bfloat16), kv_flat).astype(jnp.bfloat16)
    text_sum = lax.psum_scatter(part, "tp", scatter_dimension=0, tiled=True)
    squares = lax.psum_scatter(
        jnp.sum(wide * wide, axis=1), "tp", scatter_dimension=0, tiled=True
    )
    placed = vision_rows(
        request_len,
        token_rows,
        patch_counts,
        image_request,
        image_position,
        patches,
        vit_gain,
        merge_gain,
        rms_gain,
        qkv_weight,
        proj_weight,
        fc1_weight,
        fc2_weight,
        kv_flat,
    )
    row_ids = (
        req_index * token_rows + tp_index * share_rows + jnp.arange(share_rows, dtype=jnp.int32)
    )
    runs = patch_counts // 4
    firsts = (image_request * request_len + image_position).reshape(-1)
    offsets = row_ids[:, None] - firsts[None, :]
    taken = jnp.any((offsets >= 0) & (offsets < runs.reshape(-1)[None, :]), axis=1)
    plain = text_sum.astype(jnp.float32) * lax.rsqrt(squares[:, None] / D + epsilon)
    stacked = jnp.where(taken[:, None], placed, plain).reshape(share_rows, 2, -1)
    positions = row_ids % request_len
    live_rows = positions < request_lengths[row_ids // request_len]
    return finish_cache(stacked, positions, live_rows, kv_scale)


def solution(mesh):
    placed = (
        P(("groups", "req"), "tp"),
        P("groups", None),
        P("groups", None),
        P("groups", None),
        P("groups"),
        P(),
        P("req", None, "tp"),
        P("tp", "req"),
        P(),
        P("req", "tp"),
        P("tp", "req"),
        P(("groups", "req"), "tp"),
        P("tp"),
        P("tp", None, None),
        P(),
    )
    square = mesh.shape["req"] == SIDE and mesh.shape["tp"] == SIDE
    return jax.shard_map(
        square_body if square else general_body,
        mesh=mesh,
        in_specs=placed,
        out_specs=P(("groups", "req", "tp"), None, None),
        check_vma=False,
    )
```

```python
import functools

import jax
import jax.numpy as jnp
from jax import lax
from jax.experimental import pallas as pl
from jax.experimental.pallas import tpu as pltpu
from jax.sharding import PartitionSpec as P

VIT_HEADS = 16
VIT_HD = 80
D = 8192
KV_HEADS = 8
HEAD_DIM = 128
QGROUP = 64


epsilon = 1e-06
theta_base = 1000000.0
clip_level = 127.0


def layer_norm(values, gains):
    average = jnp.mean(values, axis=-1, keepdims=True)
    centred = values - average
    variance = jnp.mean(centred * centred, axis=-1, keepdims=True)
    return centred * lax.rsqrt(variance + epsilon) * gains


def patch_images(counts_row, patch_rows):
    bounds = jnp.cumsum(counts_row)
    row_ids = jnp.arange(patch_rows, dtype=jnp.int32)
    return jnp.sum((row_ids[:, None] >= bounds[None, :]).astype(jnp.int32), axis=1)


def attend(queries, keys_in, values_in, image_ids, factor):
    scores = (
        jnp.einsum("qhd,khd->hqk", queries, keys_in, preferred_element_type=jnp.float32) * factor
    )
    allowed = image_ids[:, None] == image_ids[None, :]
    scores = jnp.where(allowed[None], scores, -jnp.inf)
    weights = jax.nn.softmax(scores, axis=-1).astype(jnp.bfloat16)
    return jnp.einsum(
        "hqk,khd->qhd", weights, values_in, preferred_element_type=jnp.float32
    ).astype(jnp.bfloat16)


def visual_targets(patch_counts, image_request, image_position, merged_dev, request_len):
    merged_runs = patch_counts // 4
    run_ends = jnp.cumsum(merged_runs, axis=1)
    run_starts = run_ends - merged_runs
    row_ids = jnp.arange(merged_dev, dtype=jnp.int32)
    inside = (row_ids[None, :, None] >= run_starts[:, None, :]) & (
        row_ids[None, :, None] < run_ends[:, None, :]
    )
    offsets = image_request * request_len + image_position - run_starts
    target = jnp.sum(jnp.where(inside, offsets[:, None, :] + row_ids[None, :, None], 0), axis=2)
    is_live = jnp.any(inside, axis=2)
    return (target.reshape(-1), is_live.reshape(-1))


def rotate_keys(heads, positions):
    half_dim = heads.shape[-1] // 2
    frequency = theta_base ** (-2.0 * jnp.arange(half_dim, dtype=jnp.float32) / heads.shape[-1])
    angles = positions.astype(jnp.float32)[:, None] * frequency[None, :]
    cosine = jnp.cos(angles)[:, None, :]
    sine = jnp.sin(angles)[:, None, :]
    former = heads[..., :half_dim]
    latter = heads[..., half_dim:]
    return jnp.concatenate(
        [former * cosine - latter * sine, latter * cosine + former * sine], axis=-1
    )


def finish_cache(stacked, positions, live_rows, kv_scale):
    height = stacked.shape[0]
    rotated = rotate_keys(stacked[:, 0].reshape(height, KV_HEADS, HEAD_DIM), positions)
    joined = jnp.concatenate(
        [rotated.reshape(height, 1, KV_HEADS * HEAD_DIM), stacked[:, 1:2]], axis=1
    )
    bounds = jnp.repeat(clip_level * kv_scale, QGROUP, axis=1)
    clipped = jnp.clip(joined, -bounds, bounds)
    return jnp.where(live_rows[:, None, None], clipped, 0.0).astype(jnp.bfloat16)


def general_body(
    patches,
    patch_counts,
    image_request,
    image_position,
    request_lengths,
    vit_gain,
    qkv_weight,
    proj_weight,
    merge_gain,
    fc1_weight,
    fc2_weight,
    text_rows,
    rms_gain,
    kv_weight,
    kv_scale,
):
    req_devices = lax.axis_size("req")
    tp_devices = lax.axis_size("tp")
    req_index = lax.axis_index("req")
    tp_index = lax.axis_index("tp")
    patch_rows = patches.shape[0]
    merged_rows = patch_rows // 4
    token_rows = text_rows.shape[0]
    request_len = req_devices * token_rows // request_lengths.shape[0]
    local_heads = VIT_HEADS // tp_devices
    gathered = lax.all_gather(patches, "tp", axis=1, tiled=True)
    vit_width = gathered.shape[1]
    normed = layer_norm(gathered.astype(jnp.float32), vit_gain).astype(jnp.bfloat16)
    qkv_local = jnp.einsum(
        "pd,dcf->pcf",
        normed,
        lax.all_gather(qkv_weight, "req", axis=0, tiled=True),
        preferred_element_type=jnp.float32,
    ).astype(jnp.bfloat16)
    heads = qkv_local.reshape(patch_rows, 3, local_heads, VIT_HD)
    image_ids = patch_images(patch_counts[req_index], patch_rows)
    attended = attend(heads[:, 0], heads[:, 1], heads[:, 2], image_ids, VIT_HD ** (-0.5))
    flat_heads = attended.reshape(patch_rows, local_heads * VIT_HD)
    branch = jnp.dot(
        flat_heads,
        lax.all_gather(proj_weight, "req", axis=1, tiled=True),
        preferred_element_type=jnp.float32,
    )
    branch_total = lax.psum(branch, "tp")
    hidden = (gathered.astype(jnp.float32) + branch_total).astype(jnp.bfloat16)
    merged_norm = layer_norm(hidden.astype(jnp.float32), merge_gain).astype(jnp.bfloat16)
    merged = merged_norm.reshape(merged_rows, 4 * vit_width)
    feature_blocks = lax.all_to_all(merged, "req", split_axis=1, concat_axis=0, tiled=True)
    picked = feature_blocks
    before_gelu = lax.psum_scatter(
        jnp.dot(picked, fc1_weight, preferred_element_type=jnp.float32),
        "req",
        scatter_dimension=0,
        tiled=True,
    )
    activated = jax.nn.gelu(before_gelu, approximate=False).astype(jnp.bfloat16)
    outward = jnp.dot(
        lax.all_gather(activated, "req", axis=0, tiled=True),
        fc2_weight,
        preferred_element_type=jnp.float32,
    )
    target, is_live = visual_targets(
        patch_counts, image_request, image_position, merged_rows, request_len
    )
    all_rows = req_devices * token_rows
    slot_total = req_devices * merged_rows
    source_total = outward.shape[0]
    flags = (
        jnp.zeros((all_rows,), jnp.int32)
        .at[jnp.where(is_live, target, all_rows)]
        .set(1, mode="drop")
    )
    flag_grid = flags.reshape(req_devices, token_rows)
    ranks = (jnp.cumsum(flag_grid, axis=1) - flag_grid).reshape(-1)
    owners = target // token_rows
    slots = owners * merged_rows + ranks[jnp.clip(target, 0, all_rows - 1)]
    source_ids = jnp.arange(source_total, dtype=jnp.int32)
    picking = (
        jnp.full((slot_total,), source_total, jnp.int32)
        .at[jnp.where(is_live, slots, slot_total)]
        .set(source_ids, mode="drop")
    )
    padded = jnp.concatenate([outward, jnp.zeros((1, outward.shape[1]), jnp.float32)], axis=0)
    sending = padded[picking]
    arrived = lax.all_to_all(sending, "req", split_axis=0, concat_axis=1, tiled=True)
    visual = lax.psum_scatter(arrived, "tp", scatter_dimension=1, tiled=True).astype(jnp.bfloat16)
    local_flags = lax.dynamic_slice_in_dim(flags, req_index * token_rows, token_rows)
    local_ranks = lax.dynamic_slice_in_dim(ranks, req_index * token_rows, token_rows)
    chosen = visual[jnp.clip(local_ranks, 0, merged_rows - 1)]
    combined = jnp.where(local_flags[:, None] > 0, chosen, text_rows)
    wide_rows = combined.astype(jnp.float32)
    square_sums = lax.psum(jnp.sum(wide_rows * wide_rows, axis=1), "tp")
    scaled = (wide_rows * lax.rsqrt(square_sums[:, None] / D + epsilon) * rms_gain).astype(
        jnp.bfloat16
    )
    share_rows = token_rows // tp_devices
    picked = scaled
    stacked = lax.psum_scatter(
        jnp.einsum("rf,fcw->rcw", picked, kv_weight, preferred_element_type=jnp.float32),
        "tp",
        scatter_dimension=0,
        tiled=True,
    )
    row_ids = (
        req_index * token_rows + tp_index * share_rows + jnp.arange(share_rows, dtype=jnp.int32)
    )
    positions = row_ids % request_len
    live_rows = positions < request_lengths[row_ids // request_len]
    return finish_cache(stacked, positions, live_rows, kv_scale)


def iota(shape, dim):
    return lax.broadcasted_iota(jnp.int32, shape, dim)


def f32_dot(left, right):
    return jnp.dot(left, right, preferred_element_type=jnp.float32)


def image_table(counts, image_request, image_position, request_len, token_rows):
    images = []
    for s in range(counts.shape[0]):
        source = jnp.int32(s * SLOTS)
        for j in range(counts.shape[1]):
            run = counts[s, j] // 4
            first = image_request[s, j] * request_len + image_position[s, j]
            images.append((source, first, run, first // token_rows))
            source = source + run
    table = []
    for source, first, run, owner in images:
        base = jnp.int32(0)
        for _, other_first, other_run, other_owner in images:
            earlier = (other_owner == owner) & (other_first < first)
            base = base + jnp.where(earlier, other_run, 0)
        table.append((source, first, run, owner, base))
    return table


SLOTS = 16
SIDE = 4


def vision_kernel(
    request_len,
    token_rows,
    counts,
    image_request,
    image_position,
    patches,
    vit_gain,
    merge_gain,
    rms_gain,
    qkv_hbm,
    proj_hbm,
    fc1_hbm,
    fc2_hbm,
    kv_hbm,
    text_hbm,
    placed_ref,
    qkv_w,
    proj_w,
    fc1_w,
    fc2_w,
    kv_w,
    text_v,
    load_sem,
    patch_all,
    res_out,
    res_in,
    norm_out,
    norm_in,
    part_own,
    part_out,
    part_in,
    att_out,
    att_in,
    branch_out,
    branch_in,
    hid_out,
    hid_in,
    pre_own,
    pre_out,
    pre_in,
    act_out,
    act_in,
    vis_out,
    vis_in,
    row_out,
    row_in,
    sq_out,
    sq_in,
    tsq_out,
    tsq_in,
    text_keep,
    text_out,
    text_in,
    sums,
    send_sem,
    recv_sem,
):
    r = lax.axis_index("req")
    t = lax.axis_index("tp")
    rows, width = patches.shape
    full = SIDE * width

    def other(i, d):
        return lax.rem(i + d, SIDE)

    loads = []
    for k, (src, dst) in enumerate(
        (
            (qkv_hbm, qkv_w),
            (text_hbm, text_v),
            (kv_hbm, kv_w),
            (proj_hbm, proj_w),
            (fc1_hbm, fc1_w),
            (fc2_hbm, fc2_w),
        )
    ):
        copy = pltpu.make_async_copy(src, dst, load_sem.at[k])
        copy.start()
        loads.append(copy)

    barrier = pltpu.get_barrier_semaphore()
    for a in range(SIDE):
        for b in range(SIDE):
            if a or b:
                pl.semaphore_signal(
                    barrier,
                    inc=1,
                    device_id={"req": other(r, a), "tp": other(t, b)},
                    device_id_type=pl.DeviceIdType.MESH,
                )
    pl.semaphore_wait(barrier, SIDE * SIDE - 1)

    pending = []

    def remote(src, dst, stage, s_index, r_index, to_r, to_t):
        return pltpu.make_async_remote_copy(
            src_ref=src,
            dst_ref=dst,
            send_sem=send_sem.at[stage, s_index],
            recv_sem=recv_sem.at[stage, r_index],
            device_id={"req": to_r, "tp": to_t},
            device_id_type=pl.DeviceIdType.MESH,
        )

    def send(copy, unless=None):
        if unless is None:
            copy.start()
            pending.append(copy.wait_send)
        else:
            pl.when(jnp.logical_not(unless))(copy.start)
            pending.append(lambda: pl.when(jnp.logical_not(unless))(copy.wait_send))

    def receive(dst, stage, index, unless=None):
        copy = remote(dst, dst, stage, 0, index, other(r, 1), t)
        if unless is None:
            copy.wait_recv()
        else:
            pl.when(jnp.logical_not(unless))(copy.wait_recv)

    on_diagonal = r == t

    for d in range(1, SIDE):
        send(remote(patches, patch_all.at[t], 0, d, d, r, other(t, d)))
    patch_all[t] = patches[...]
    picks_i = iota((rows, rows), 0)
    picks_j = iota((rows, rows), 1)
    by_class = jnp.where(
        picks_j == 4 * lax.rem(picks_i, SLOTS) + picks_i // SLOTS, 1.0, 0.0
    ).astype(jnp.bfloat16)
    regrouped = f32_dot(by_class, patches[...]).astype(jnp.bfloat16)
    for c in range(SIDE):
        res_out[c] = regrouped[c * SLOTS : (c + 1) * SLOTS]
    for d in range(SIDE):
        c = other(t, d)
        unless = on_diagonal if d == 0 else None
        send(remote(res_out.at[c], res_in.at[r], 1, d, r, t, c), unless)

    @pl.when(on_diagonal)
    def _():
        res_in[r] = res_out[t]

    share = placed_ref.shape[0]

    def text_chunk(c):
        return text_v[pl.ds(pl.multiple_of(c * share, share), share)].astype(jnp.float32)

    loads[1].wait()
    for c in range(SIDE):
        wide = text_chunk(c)
        column = jnp.sum(wide * wide, axis=1, keepdims=True)
        tsq_out[c] = jnp.transpose(jnp.broadcast_to(column, (share, share)))[:8]
    for d in range(1, SIDE):
        send(remote(tsq_out, tsq_in.at[d - 1], 12, d, d, r, other(t, d)))
    for d in range(1, SIDE):
        receive(patch_all.at[other(t, SIDE - d)], 0, d)

    def chunk_norm(values, gains):
        total = jnp.sum(values[0], axis=1, keepdims=True)
        for v in values[1:]:
            total = total + jnp.sum(v, axis=1, keepdims=True)
        average = total / full
        centred = [v - average for v in values]
        total = jnp.sum(centred[0] * centred[0], axis=1, keepdims=True)
        for v in centred[1:]:
            total = total + jnp.sum(v * v, axis=1, keepdims=True)
        inverse = lax.rsqrt(total / full + epsilon)
        return [
            (v * inverse * gains[c : c + 1, :]).astype(jnp.bfloat16)
            for c, v in enumerate(centred)
        ]

    normed = chunk_norm([patch_all[c].astype(jnp.float32) for c in range(SIDE)], vit_gain)
    for c in range(SIDE):
        norm_out[c] = normed[c]
    for d in range(1, SIDE):
        p = other(r, d)
        send(remote(norm_out.at[p], norm_in.at[r], 2, d, d, p, t))
    norm_in[r] = norm_out[r]
    for d in range(1, SIDE):
        receive(norm_in.at[other(r, SIDE - d)], 2, d)

    loads[0].wait()
    every = norm_in[...].reshape(SIDE * rows, width)
    for c in range(3):
        part = f32_dot(every, qkv_w[c]).reshape(SIDE, rows, width)
        part_own[:, c] = part
        part_out[:, c] = part.astype(jnp.bfloat16)
    for d in range(1, SIDE):
        p = other(r, d)
        send(remote(part_out.at[p], part_in.at[d - 1], 3, d, d, p, t))

    for d in range(1, SIDE):
        receive(tsq_in.at[d - 1], 12, d)
    for c in range(SIDE):
        tsq_out_sum = tsq_out[c]
        for d in range(1, SIDE):
            tsq_out_sum = tsq_out_sum + tsq_in[d - 1, c]
        sums[c] = tsq_out_sum
    loads[2].wait()
    mate = t + 1 - 2 * lax.rem(t, 2)
    across = other(t, 2)
    columns = text_v.shape[1]

    def text_part(c):
        squares = jnp.transpose(jnp.broadcast_to(sums[c][:1], (share, share)))[:, :1]
        inverse = lax.rsqrt(squares / (SIDE * columns) + epsilon)
        scaled = (text_chunk(c) * inverse * rms_gain[...]).astype(jnp.bfloat16)
        return f32_dot(scaled, kv_w[...])

    text_out[0] = text_part(other(mate, 2)).astype(jnp.bfloat16)
    send(remote(text_out.at[0], text_in.at[0], 13, 0, 0, r, mate))
    text_keep[...] = text_part(across)
    receive(text_in.at[0], 13, 0)
    text_out[1] = (text_keep[...] + text_in[0].astype(jnp.float32)).astype(jnp.bfloat16)
    send(remote(text_out.at[1], text_in.at[1], 13, 1, 1, r, across))

    total = part_own[r]
    for d in range(1, SIDE):
        receive(part_in.at[d - 1], 3, d)
        total = total + part_in[d - 1].astype(jnp.float32)
    qkv = total.astype(jnp.bfloat16)

    first_end = counts[r, 0]
    second_end = first_end + counts[r, 1]

    def ids(index):
        return (index >= first_end).astype(jnp.int32) + (index >= second_end).astype(jnp.int32)

    allowed = ids(picks_i) == ids(picks_j)
    lanes = iota((rows, width), 1) // VIT_HD
    attended = jnp.zeros((rows, width), jnp.float32)
    for h in range(width // VIT_HD):
        mine = lanes == h
        query = jnp.where(mine, qkv[0].astype(jnp.float32), 0.0).astype(jnp.bfloat16)
        value = jnp.where(mine, qkv[2].astype(jnp.float32), 0.0).astype(jnp.bfloat16)
        scores = lax.dot_general(
            query, qkv[1], (((1,), (1,)), ((), ())), preferred_element_type=jnp.float32
        ) * (VIT_HD ** (-0.5))
        scores = jnp.where(allowed, scores, -jnp.inf)
        weights = jnp.exp(scores - jnp.max(scores, axis=1, keepdims=True))
        weights = weights / jnp.sum(weights, axis=1, keepdims=True)
        attended = attended + f32_dot(weights.astype(jnp.bfloat16), value)
    att_out[...] = f32_dot(by_class, attended.astype(jnp.bfloat16)).astype(jnp.bfloat16)
    for d in range(1, SIDE):
        send(remote(att_out, att_in.at[r], 4, d, d, other(r, d), t))
    att_in[r] = att_out[...]
    text_out[2] = text_part(mate).astype(jnp.bfloat16)
    send(remote(text_out.at[2], text_in.at[2], 13, 2, 2, r, mate))
    loads[3].wait()
    for d in range(1, SIDE):
        receive(att_in.at[other(r, SIDE - d)], 4, d)

    branch = f32_dot(att_in[...].reshape(SIDE * rows, width), proj_w[...])
    branch = branch.reshape(SIDE, SIDE, SLOTS, width)
    for c in range(SIDE):
        branch_out[c] = branch[:, c].reshape(rows, width)
    for d in range(1, SIDE):
        c = other(t, d)
        send(remote(branch_out.at[c], branch_in.at[d - 1], 5, d, d, r, c))
    total = branch_out[t]
    for d in range(SIDE):
        q = other(r, d)
        receive(res_in.at[q], 1, q, on_diagonal if d == 0 else None)
    residual = res_in[...].reshape(rows, width).astype(jnp.float32)
    for d in range(1, SIDE):
        receive(branch_in.at[d - 1], 5, d)
        total = total + branch_in[d - 1]
    hid_out[...] = (residual + total).astype(jnp.bfloat16)
    for d in range(SIDE):
        unless = on_diagonal if d == 0 else None
        send(remote(hid_out, hid_in.at[r], 6, d, r, t, other(t, d)), unless)

    @pl.when(on_diagonal)
    def _():
        hid_in[r] = hid_out[...]

    text_keep[...] = text_part(t)
    loads[4].wait()
    for d in range(SIDE):
        q = other(r, d)
        receive(hid_in.at[q], 6, q, on_diagonal if d == 0 else None)

    merged = chunk_norm([hid_in[c].astype(jnp.float32) for c in range(SIDE)], merge_gain)
    before = f32_dot(merged[0], fc1_w[0:width])
    for c in range(1, SIDE):
        before = before + f32_dot(merged[c], fc1_w[c * width : (c + 1) * width])
    for q in range(SIDE):
        pre_own[q] = before[q * SLOTS : (q + 1) * SLOTS]
        pre_out[q] = before[q * SLOTS : (q + 1) * SLOTS].astype(jnp.bfloat16)
    for d in range(1, SIDE):
        p = other(r, d)
        send(remote(pre_out.at[p], pre_in.at[d - 1], 7, d, d, p, t))
    total = pre_own[r]
    for d in range(1, SIDE):
        receive(pre_in.at[d - 1], 7, d)
        total = total + pre_in[d - 1].astype(jnp.float32)
    act_out[...] = (0.5 * total * (1.0 + lax.erf(total * (0.5**0.5)))).astype(jnp.bfloat16)
    for d in range(1, SIDE):
        send(remote(act_out, act_in.at[r], 8, d, d, other(r, d), t))
    act_in[r] = act_out[...]
    table = image_table(counts, image_request, image_position, request_len, token_rows)
    slot_i = iota((SIDE * SLOTS, SIDE * SLOTS), 0)
    row_j = iota((SIDE * SLOTS, SIDE * SLOTS), 1)
    pick = jnp.zeros(slot_i.shape, jnp.float32)
    for source, _, run, owner, base in table:
        offset = row_j - source
        hit = (slot_i - (owner * SLOTS + base) == offset) & (offset >= 0) & (offset < run)
        pick = jnp.where(hit, 1.0, pick)
    pick = pick.astype(jnp.bfloat16)
    loads[5].wait()
    for d in range(1, SIDE):
        receive(act_in.at[other(r, SIDE - d)], 8, d)

    active = act_in[...].reshape(SIDE * SLOTS, act_in.shape[2])
    picked = f32_dot(pick, active).astype(jnp.bfloat16)
    outward = f32_dot(picked, fc2_w[...]).astype(jnp.bfloat16)
    for q in range(SIDE):
        vis_out[q] = outward[q * SLOTS : (q + 1) * SLOTS]
    for d in range(SIDE):
        q = other(r, d)
        unless = on_diagonal if d == 0 else None
        send(remote(vis_out.at[q], vis_in.at[t], 9, d, t, q, r), unless)

    @pl.when(on_diagonal)
    def _():
        vis_in[t] = vis_out[r]

    for d in range(SIDE):
        q = other(t, d)
        receive(vis_in.at[q], 9, q, on_diagonal if d == 0 else None)
    visual = vis_in[0].astype(jnp.float32)
    for q in range(1, SIDE):
        visual = visual + vis_in[q].astype(jnp.float32)
    visual = visual.astype(jnp.bfloat16).astype(jnp.float32)
    squares = jnp.sum(visual * visual, axis=1, keepdims=True)
    sq_out[...] = jnp.broadcast_to(squares, sq_out.shape)
    for d in range(1, SIDE):
        send(remote(sq_out, sq_in.at[d - 1], 10, d, d, r, other(t, d)))
    projected = f32_dot((visual * rms_gain[...]).astype(jnp.bfloat16), kv_w[...])
    row_out[...] = projected.astype(jnp.bfloat16)
    for d in range(1, SIDE):
        send(remote(row_out, row_in.at[d - 1], 11, d, d, r, other(t, d)))
    total = projected
    squares = sq_out[...]
    for d in range(1, SIDE):
        receive(sq_in.at[d - 1], 10, d)
        squares = squares + sq_in[d - 1]
        receive(row_in.at[d - 1], 11, d)
        total = total + row_in[d - 1].astype(jnp.float32)
    total = total * lax.rsqrt(squares[:, :1] / (SIDE * visual.shape[1]) + epsilon)
    place_i = iota((share, SLOTS), 0) + r * token_rows + t * share
    place_k = iota((share, SLOTS), 1)
    place = jnp.zeros((share, SLOTS), jnp.float32)
    for _, first, run, owner, base in table:
        offset = place_i - first
        hit = (owner == r) & (place_k - base == offset) & (offset >= 0) & (offset < run)
        place = jnp.where(hit, 1.0, place)
    placed = jnp.dot(
        place, total, preferred_element_type=jnp.float32, precision=lax.Precision.HIGHEST
    )
    taken = jnp.sum(place, axis=1, keepdims=True) > 0.5
    plain = text_keep[...]
    for k in (1, 2):
        receive(text_in.at[k], 13, k)
        plain = plain + text_in[k].astype(jnp.float32)
    placed_ref[...] = jnp.where(taken, placed, plain)
    for wait in pending:
        wait()


def vision_rows(
    request_len,
    token_rows,
    patch_counts,
    image_request,
    image_position,
    patches,
    vit_gain,
    merge_gain,
    rms_gain,
    qkv_weight,
    proj_weight,
    fc1_weight,
    fc2_weight,
    kv_flat,
    text_rows,
):
    rows, width = patches.shape
    hidden_w = fc1_weight.shape[1]
    share_w, kv_width = kv_flat.shape
    bf16, f32 = jnp.bfloat16, jnp.float32
    n = SIDE
    share = token_rows // n
    smem = pl.BlockSpec(memory_space=pltpu.SMEM)
    vmem = pl.BlockSpec(memory_space=pltpu.VMEM)
    anywhere = pl.BlockSpec(memory_space=pl.ANY)
    buffers = [
        ((3, width, width), bf16),
        (proj_weight.shape, bf16),
        (fc1_weight.shape, bf16),
        (fc2_weight.shape, bf16),
        (kv_flat.shape, bf16),
        (text_rows.shape, bf16),
        None,
        ((n, rows, width), bf16),
        ((n, SLOTS, width), bf16),
        ((n, SLOTS, width), bf16),
        ((n, rows, width), bf16),
        ((n, rows, width), bf16),
        ((n, 3, rows, width), f32),
        ((n, 3, rows, width), bf16),
        ((n - 1, 3, rows, width), bf16),
        ((rows, width), bf16),
        ((n, rows, width), bf16),
        ((n, rows, width), f32),
        ((n - 1, rows, width), f32),
        ((rows, width), bf16),
        ((n, rows, width), bf16),
        ((n, SLOTS, hidden_w), f32),
        ((n, SLOTS, hidden_w), bf16),
        ((n - 1, SLOTS, hidden_w), bf16),
        ((SLOTS, hidden_w), bf16),
        ((n, SLOTS, hidden_w), bf16),
        ((n, SLOTS, share_w), bf16),
        ((n, SLOTS, share_w), bf16),
        ((SLOTS, kv_width), bf16),
        ((n - 1, SLOTS, kv_width), bf16),
        ((SLOTS, 128), f32),
        ((n - 1, SLOTS, 128), f32),
        ((n, 8, share), f32),
        ((n - 1, n, 8, share), f32),
        ((share, kv_width), f32),
        ((3, share, kv_width), bf16),
        ((3, share, kv_width), bf16),
        ((n, 8, share), f32),
    ]
    scratch = [
        pltpu.SemaphoreType.DMA((6,)) if b is None else pltpu.VMEM(*b) for b in buffers
    ] + [pltpu.SemaphoreType.DMA((14, n)), pltpu.SemaphoreType.DMA((14, n))]
    return pl.pallas_call(
        functools.partial(vision_kernel, request_len, token_rows),
        out_shape=jax.ShapeDtypeStruct((token_rows // n, kv_width), f32),
        in_specs=[smem] * 3 + [vmem] * 4 + [anywhere] * 6,
        out_specs=vmem,
        scratch_shapes=scratch,
        compiler_params=pltpu.CompilerParams(
            collective_id=0, has_side_effects=True, vmem_limit_bytes=48 * 1024 * 1024
        ),
        cost_estimate=pl.CostEstimate(
            flops=6 * 10**9, bytes_accessed=22 * 10**6, transcendentals=10**5
        ),
    )(
        patch_counts,
        image_request,
        image_position,
        patches,
        vit_gain.reshape(n, width),
        merge_gain.reshape(n, width),
        rms_gain.reshape(1, share_w),
        jnp.transpose(qkv_weight, (1, 0, 2)),
        proj_weight,
        fc1_weight,
        fc2_weight,
        kv_flat,
        text_rows,
    )


def square_body(
    patches,
    patch_counts,
    image_request,
    image_position,
    request_lengths,
    vit_gain,
    qkv_weight,
    proj_weight,
    merge_gain,
    fc1_weight,
    fc2_weight,
    text_rows,
    rms_gain,
    kv_weight,
    kv_scale,
):
    req_index = lax.axis_index("req")
    tp_index = lax.axis_index("tp")
    token_rows, share_w = text_rows.shape
    request_len = SIDE * token_rows // request_lengths.shape[0]
    share_rows = token_rows // SIDE
    kv_flat = kv_weight.reshape(share_w, -1)
    placed = vision_rows(
        request_len,
        token_rows,
        patch_counts,
        image_request,
        image_position,
        patches,
        vit_gain,
        merge_gain,
        rms_gain,
        qkv_weight,
        proj_weight,
        fc1_weight,
        fc2_weight,
        kv_flat,
        text_rows,
    )
    row_ids = (
        req_index * token_rows + tp_index * share_rows + jnp.arange(share_rows, dtype=jnp.int32)
    )
    stacked = placed.reshape(share_rows, 2, -1)
    positions = row_ids % request_len
    live_rows = positions < request_lengths[row_ids // request_len]
    return finish_cache(stacked, positions, live_rows, kv_scale)


def solution(mesh):
    placed = (
        P(("groups", "req"), "tp"),
        P("groups", None),
        P("groups", None),
        P("groups", None),
        P("groups"),
        P(),
        P("req", None, "tp"),
        P("tp", "req"),
        P(),
        P("req", "tp"),
        P("tp", "req"),
        P(("groups", "req"), "tp"),
        P("tp"),
        P("tp", None, None),
        P(),
    )
    square = mesh.shape["req"] == SIDE and mesh.shape["tp"] == SIDE
    return jax.shard_map(
        square_body if square else general_body,
        mesh=mesh,
        in_specs=placed,
        out_specs=P(("groups", "req", "tp"), None, None),
        check_vma=False,
    )
```

```python
import functools

import jax
import jax.numpy as jnp
from jax import lax
from jax.experimental import pallas as pl
from jax.experimental.pallas import tpu as pltpu
from jax.sharding import PartitionSpec as P

VIT_HEADS = 16
VIT_HD = 80
D = 8192
KV_HEADS = 8
HEAD_DIM = 128
QGROUP = 64


epsilon = 1e-06
theta_base = 1000000.0
clip_level = 127.0


def layer_norm(values, gains):
    average = jnp.mean(values, axis=-1, keepdims=True)
    centred = values - average
    variance = jnp.mean(centred * centred, axis=-1, keepdims=True)
    return centred * lax.rsqrt(variance + epsilon) * gains


def patch_images(counts_row, patch_rows):
    bounds = jnp.cumsum(counts_row)
    row_ids = jnp.arange(patch_rows, dtype=jnp.int32)
    return jnp.sum((row_ids[:, None] >= bounds[None, :]).astype(jnp.int32), axis=1)


def attend(queries, keys_in, values_in, image_ids, factor):
    scores = (
        jnp.einsum("qhd,khd->hqk", queries, keys_in, preferred_element_type=jnp.float32) * factor
    )
    allowed = image_ids[:, None] == image_ids[None, :]
    scores = jnp.where(allowed[None], scores, -jnp.inf)
    weights = jax.nn.softmax(scores, axis=-1).astype(jnp.bfloat16)
    return jnp.einsum(
        "hqk,khd->qhd", weights, values_in, preferred_element_type=jnp.float32
    ).astype(jnp.bfloat16)


def visual_targets(patch_counts, image_request, image_position, merged_dev, request_len):
    merged_runs = patch_counts // 4
    run_ends = jnp.cumsum(merged_runs, axis=1)
    run_starts = run_ends - merged_runs
    row_ids = jnp.arange(merged_dev, dtype=jnp.int32)
    inside = (row_ids[None, :, None] >= run_starts[:, None, :]) & (
        row_ids[None, :, None] < run_ends[:, None, :]
    )
    offsets = image_request * request_len + image_position - run_starts
    target = jnp.sum(jnp.where(inside, offsets[:, None, :] + row_ids[None, :, None], 0), axis=2)
    is_live = jnp.any(inside, axis=2)
    return (target.reshape(-1), is_live.reshape(-1))


def rotate_keys(heads, positions):
    half_dim = heads.shape[-1] // 2
    frequency = theta_base ** (-2.0 * jnp.arange(half_dim, dtype=jnp.float32) / heads.shape[-1])
    angles = positions.astype(jnp.float32)[:, None] * frequency[None, :]
    cosine = jnp.cos(angles)[:, None, :]
    sine = jnp.sin(angles)[:, None, :]
    former = heads[..., :half_dim]
    latter = heads[..., half_dim:]
    return jnp.concatenate(
        [former * cosine - latter * sine, latter * cosine + former * sine], axis=-1
    )


def finish_cache(stacked, positions, live_rows, kv_scale):
    height = stacked.shape[0]
    rotated = rotate_keys(stacked[:, 0].reshape(height, KV_HEADS, HEAD_DIM), positions)
    joined = jnp.concatenate(
        [rotated.reshape(height, 1, KV_HEADS * HEAD_DIM), stacked[:, 1:2]], axis=1
    )
    bounds = jnp.repeat(clip_level * kv_scale, QGROUP, axis=1)
    clipped = jnp.clip(joined, -bounds, bounds)
    return jnp.where(live_rows[:, None, None], clipped, 0.0).astype(jnp.bfloat16)


def general_body(
    patches,
    patch_counts,
    image_request,
    image_position,
    request_lengths,
    vit_gain,
    qkv_weight,
    proj_weight,
    merge_gain,
    fc1_weight,
    fc2_weight,
    text_rows,
    rms_gain,
    kv_weight,
    kv_scale,
):
    req_devices = lax.axis_size("req")
    tp_devices = lax.axis_size("tp")
    req_index = lax.axis_index("req")
    tp_index = lax.axis_index("tp")
    patch_rows = patches.shape[0]
    merged_rows = patch_rows // 4
    token_rows = text_rows.shape[0]
    request_len = req_devices * token_rows // request_lengths.shape[0]
    local_heads = VIT_HEADS // tp_devices
    gathered = lax.all_gather(patches, "tp", axis=1, tiled=True)
    vit_width = gathered.shape[1]
    normed = layer_norm(gathered.astype(jnp.float32), vit_gain).astype(jnp.bfloat16)
    qkv_local = jnp.einsum(
        "pd,dcf->pcf",
        normed,
        lax.all_gather(qkv_weight, "req", axis=0, tiled=True),
        preferred_element_type=jnp.float32,
    ).astype(jnp.bfloat16)
    heads = qkv_local.reshape(patch_rows, 3, local_heads, VIT_HD)
    image_ids = patch_images(patch_counts[req_index], patch_rows)
    attended = attend(heads[:, 0], heads[:, 1], heads[:, 2], image_ids, VIT_HD ** (-0.5))
    flat_heads = attended.reshape(patch_rows, local_heads * VIT_HD)
    branch = jnp.dot(
        flat_heads,
        lax.all_gather(proj_weight, "req", axis=1, tiled=True),
        preferred_element_type=jnp.float32,
    )
    branch_total = lax.psum(branch, "tp")
    hidden = (gathered.astype(jnp.float32) + branch_total).astype(jnp.bfloat16)
    merged_norm = layer_norm(hidden.astype(jnp.float32), merge_gain).astype(jnp.bfloat16)
    merged = merged_norm.reshape(merged_rows, 4 * vit_width)
    feature_blocks = lax.all_to_all(merged, "req", split_axis=1, concat_axis=0, tiled=True)
    picked = feature_blocks
    before_gelu = lax.psum_scatter(
        jnp.dot(picked, fc1_weight, preferred_element_type=jnp.float32),
        "req",
        scatter_dimension=0,
        tiled=True,
    )
    activated = jax.nn.gelu(before_gelu, approximate=False).astype(jnp.bfloat16)
    outward = jnp.dot(
        lax.all_gather(activated, "req", axis=0, tiled=True),
        fc2_weight,
        preferred_element_type=jnp.float32,
    )
    target, is_live = visual_targets(
        patch_counts, image_request, image_position, merged_rows, request_len
    )
    all_rows = req_devices * token_rows
    slot_total = req_devices * merged_rows
    source_total = outward.shape[0]
    flags = (
        jnp.zeros((all_rows,), jnp.int32)
        .at[jnp.where(is_live, target, all_rows)]
        .set(1, mode="drop")
    )
    flag_grid = flags.reshape(req_devices, token_rows)
    ranks = (jnp.cumsum(flag_grid, axis=1) - flag_grid).reshape(-1)
    owners = target // token_rows
    slots = owners * merged_rows + ranks[jnp.clip(target, 0, all_rows - 1)]
    source_ids = jnp.arange(source_total, dtype=jnp.int32)
    picking = (
        jnp.full((slot_total,), source_total, jnp.int32)
        .at[jnp.where(is_live, slots, slot_total)]
        .set(source_ids, mode="drop")
    )
    padded = jnp.concatenate([outward, jnp.zeros((1, outward.shape[1]), jnp.float32)], axis=0)
    sending = padded[picking]
    arrived = lax.all_to_all(sending, "req", split_axis=0, concat_axis=1, tiled=True)
    visual = lax.psum_scatter(arrived, "tp", scatter_dimension=1, tiled=True).astype(jnp.bfloat16)
    local_flags = lax.dynamic_slice_in_dim(flags, req_index * token_rows, token_rows)
    local_ranks = lax.dynamic_slice_in_dim(ranks, req_index * token_rows, token_rows)
    chosen = visual[jnp.clip(local_ranks, 0, merged_rows - 1)]
    combined = jnp.where(local_flags[:, None] > 0, chosen, text_rows)
    wide_rows = combined.astype(jnp.float32)
    square_sums = lax.psum(jnp.sum(wide_rows * wide_rows, axis=1), "tp")
    scaled = (wide_rows * lax.rsqrt(square_sums[:, None] / D + epsilon) * rms_gain).astype(
        jnp.bfloat16
    )
    share_rows = token_rows // tp_devices
    picked = scaled
    stacked = lax.psum_scatter(
        jnp.einsum("rf,fcw->rcw", picked, kv_weight, preferred_element_type=jnp.float32),
        "tp",
        scatter_dimension=0,
        tiled=True,
    )
    row_ids = (
        req_index * token_rows + tp_index * share_rows + jnp.arange(share_rows, dtype=jnp.int32)
    )
    positions = row_ids % request_len
    live_rows = positions < request_lengths[row_ids // request_len]
    return finish_cache(stacked, positions, live_rows, kv_scale)


def iota(shape, dim):
    return lax.broadcasted_iota(jnp.int32, shape, dim)


def f32_dot(left, right):
    return jnp.dot(left, right, preferred_element_type=jnp.float32)


def image_table(counts, image_request, image_position, request_len, token_rows):
    images = []
    for s in range(counts.shape[0]):
        source = jnp.int32(s * SLOTS)
        for j in range(counts.shape[1]):
            run = counts[s, j] // 4
            first = image_request[s, j] * request_len + image_position[s, j]
            images.append((source, first, run, first // token_rows))
            source = source + run
    table = []
    for source, first, run, owner in images:
        base = jnp.int32(0)
        for _, other_first, other_run, other_owner in images:
            earlier = (other_owner == owner) & (other_first < first)
            base = base + jnp.where(earlier, other_run, 0)
        table.append((source, first, run, owner, base))
    return table


SLOTS = 16
SIDE = 4


def cell_kernel(
    request_len,
    token_rows,
    tables,
    lengths,
    patches,
    vit_gain,
    merge_gain,
    rms_gain,
    cosines,
    sines,
    limits,
    qkv_hbm,
    proj_hbm,
    fc1_hbm,
    fc2_hbm,
    kv_hbm,
    text_hbm,
    cache_ref,
    qkv_w,
    proj_w,
    fc1_w,
    fc2_w,
    kv_w,
    text_v,
    load_sem,
    patch_all,
    res_out,
    res_in,
    norm_out,
    norm_in,
    part_own,
    part_out,
    part_in,
    att_out,
    att_in,
    branch_out,
    branch_in,
    hid_out,
    hid_in,
    pre_own,
    pre_out,
    pre_in,
    act_out,
    act_in,
    vis_out,
    vis_in,
    row_out,
    row_in,
    sq_out,
    sq_in,
    tsq_out,
    tsq_in,
    text_keep,
    text_out,
    text_in,
    sums,
    send_sem,
    recv_sem,
):
    r = lax.axis_index("req")
    t = lax.axis_index("tp")
    rows, width = patches.shape
    full = SIDE * width
    counts, image_request, image_position = (tables.at[k] for k in range(3))

    def other(i, d):
        return lax.rem(i + d, SIDE)

    loads = []
    for k, (src, dst) in enumerate(
        (
            (qkv_hbm, qkv_w),
            (text_hbm, text_v),
            (kv_hbm, kv_w),
            (proj_hbm, proj_w),
            (fc1_hbm, fc1_w),
            (fc2_hbm, fc2_w),
        )
    ):
        copy = pltpu.make_async_copy(src, dst, load_sem.at[k])
        copy.start()
        loads.append(copy)

    barrier = pltpu.get_barrier_semaphore()
    for a in range(SIDE):
        for b in range(SIDE):
            if a or b:
                pl.semaphore_signal(
                    barrier,
                    inc=1,
                    device_id={"req": other(r, a), "tp": other(t, b)},
                    device_id_type=pl.DeviceIdType.MESH,
                )
    pl.semaphore_wait(barrier, SIDE * SIDE - 1)

    pending = []

    def remote(src, dst, stage, s_index, r_index, to_r, to_t):
        return pltpu.make_async_remote_copy(
            src_ref=src,
            dst_ref=dst,
            send_sem=send_sem.at[stage, s_index],
            recv_sem=recv_sem.at[stage, r_index],
            device_id={"req": to_r, "tp": to_t},
            device_id_type=pl.DeviceIdType.MESH,
        )

    def send(copy, unless=None):
        if unless is None:
            copy.start()
            pending.append(copy.wait_send)
        else:
            pl.when(jnp.logical_not(unless))(copy.start)
            pending.append(lambda: pl.when(jnp.logical_not(unless))(copy.wait_send))

    def receive(dst, stage, index, unless=None):
        copy = remote(dst, dst, stage, 0, index, other(r, 1), t)
        if unless is None:
            copy.wait_recv()
        else:
            pl.when(jnp.logical_not(unless))(copy.wait_recv)

    on_diagonal = r == t

    for d in range(1, SIDE):
        send(remote(patches, patch_all.at[t], 0, d, d, r, other(t, d)))
    patch_all[t] = patches[...]
    picks_i = iota((rows, rows), 0)
    picks_j = iota((rows, rows), 1)
    by_class = jnp.where(
        picks_j == 4 * lax.rem(picks_i, SLOTS) + picks_i // SLOTS, 1.0, 0.0
    ).astype(jnp.bfloat16)
    regrouped = f32_dot(by_class, patches[...]).astype(jnp.bfloat16)
    for c in range(SIDE):
        res_out[c] = regrouped[c * SLOTS : (c + 1) * SLOTS]
    for d in range(SIDE):
        c = other(t, d)
        unless = on_diagonal if d == 0 else None
        send(remote(res_out.at[c], res_in.at[r], 1, d, r, t, c), unless)

    @pl.when(on_diagonal)
    def _():
        res_in[r] = res_out[t]

    share = cache_ref.shape[0]

    def text_chunk(c):
        return text_v[pl.ds(pl.multiple_of(c * share, share), share)].astype(jnp.float32)

    loads[1].wait()
    for c in range(SIDE):
        wide = text_chunk(c)
        column = jnp.sum(wide * wide, axis=1, keepdims=True)
        tsq_out[c] = jnp.transpose(jnp.broadcast_to(column, (share, share)))[:8]
    for d in range(1, SIDE):
        send(remote(tsq_out, tsq_in.at[d - 1], 12, d, d, r, other(t, d)))
    for d in range(1, SIDE):
        receive(patch_all.at[other(t, SIDE - d)], 0, d)

    def chunk_norm(values, gains):
        total = jnp.sum(values[0], axis=1, keepdims=True)
        for v in values[1:]:
            total = total + jnp.sum(v, axis=1, keepdims=True)
        average = total / full
        centred = [v - average for v in values]
        total = jnp.sum(centred[0] * centred[0], axis=1, keepdims=True)
        for v in centred[1:]:
            total = total + jnp.sum(v * v, axis=1, keepdims=True)
        inverse = lax.rsqrt(total / full + epsilon)
        return [
            (v * inverse * gains[:, c * width : (c + 1) * width]).astype(jnp.bfloat16)
            for c, v in enumerate(centred)
        ]

    normed = chunk_norm([patch_all[c].astype(jnp.float32) for c in range(SIDE)], vit_gain)
    for c in range(SIDE):
        norm_out[c] = normed[c]
    for d in range(1, SIDE):
        p = other(r, d)
        send(remote(norm_out.at[p], norm_in.at[r], 2, d, d, p, t))
    norm_in[r] = norm_out[r]
    for d in range(1, SIDE):
        receive(norm_in.at[other(r, SIDE - d)], 2, d)

    loads[0].wait()
    every = norm_in[...].reshape(SIDE * rows, width)
    for c in range(3):
        part = f32_dot(every, qkv_w[c]).reshape(SIDE, rows, width)
        part_own[:, c] = part
        part_out[:, c] = part.astype(jnp.bfloat16)
    for d in range(1, SIDE):
        p = other(r, d)
        send(remote(part_out.at[p], part_in.at[d - 1], 3, d, d, p, t))

    for d in range(1, SIDE):
        receive(tsq_in.at[d - 1], 12, d)
    for c in range(SIDE):
        tsq_out_sum = tsq_out[c]
        for d in range(1, SIDE):
            tsq_out_sum = tsq_out_sum + tsq_in[d - 1, c]
        sums[c] = tsq_out_sum
    loads[2].wait()
    mate = t + 1 - 2 * lax.rem(t, 2)
    across = other(t, 2)
    columns = text_v.shape[1]

    def text_part(c):
        squares = jnp.transpose(jnp.broadcast_to(sums[c][:1], (share, share)))[:, :1]
        inverse = lax.rsqrt(squares / (SIDE * columns) + epsilon)
        scaled = (text_chunk(c) * inverse * rms_gain[...]).astype(jnp.bfloat16)
        return f32_dot(scaled, kv_w[...])

    text_out[0] = text_part(other(mate, 2)).astype(jnp.bfloat16)
    send(remote(text_out.at[0], text_in.at[0], 13, 0, 0, r, mate))
    text_keep[...] = text_part(across)
    receive(text_in.at[0], 13, 0)
    text_out[1] = (text_keep[...] + text_in[0].astype(jnp.float32)).astype(jnp.bfloat16)
    send(remote(text_out.at[1], text_in.at[1], 13, 1, 1, r, across))

    total = part_own[r]
    for d in range(1, SIDE):
        receive(part_in.at[d - 1], 3, d)
        total = total + part_in[d - 1].astype(jnp.float32)
    qkv = total.astype(jnp.bfloat16)

    first_end = counts[r, 0]
    second_end = first_end + counts[r, 1]

    def ids(index):
        return (index >= first_end).astype(jnp.int32) + (index >= second_end).astype(jnp.int32)

    allowed = ids(picks_i) == ids(picks_j)
    lanes = iota((rows, width), 1) // VIT_HD
    attended = jnp.zeros((rows, width), jnp.float32)
    for h in range(width // VIT_HD):
        mine = lanes == h
        query = jnp.where(mine, qkv[0].astype(jnp.float32), 0.0).astype(jnp.bfloat16)
        value = jnp.where(mine, qkv[2].astype(jnp.float32), 0.0).astype(jnp.bfloat16)
        scores = lax.dot_general(
            query, qkv[1], (((1,), (1,)), ((), ())), preferred_element_type=jnp.float32
        ) * (VIT_HD ** (-0.5))
        scores = jnp.where(allowed, scores, -jnp.inf)
        weights = jnp.exp(scores - jnp.max(scores, axis=1, keepdims=True))
        weights = weights / jnp.sum(weights, axis=1, keepdims=True)
        attended = attended + f32_dot(weights.astype(jnp.bfloat16), value)
    att_out[...] = f32_dot(by_class, attended.astype(jnp.bfloat16)).astype(jnp.bfloat16)
    for d in range(1, SIDE):
        send(remote(att_out, att_in.at[r], 4, d, d, other(r, d), t))
    att_in[r] = att_out[...]
    text_out[2] = text_part(mate).astype(jnp.bfloat16)
    send(remote(text_out.at[2], text_in.at[2], 13, 2, 2, r, mate))
    loads[3].wait()
    for d in range(1, SIDE):
        receive(att_in.at[other(r, SIDE - d)], 4, d)

    branch = f32_dot(att_in[...].reshape(SIDE * rows, width), proj_w[...])
    branch = branch.reshape(SIDE, SIDE, SLOTS, width)
    for c in range(SIDE):
        branch_out[c] = branch[:, c].reshape(rows, width)
    for d in range(1, SIDE):
        c = other(t, d)
        send(remote(branch_out.at[c], branch_in.at[d - 1], 5, d, d, r, c))
    total = branch_out[t]
    for d in range(SIDE):
        q = other(r, d)
        receive(res_in.at[q], 1, q, on_diagonal if d == 0 else None)
    residual = res_in[...].reshape(rows, width).astype(jnp.float32)
    for d in range(1, SIDE):
        receive(branch_in.at[d - 1], 5, d)
        total = total + branch_in[d - 1]
    hid_out[...] = (residual + total).astype(jnp.bfloat16)
    for d in range(SIDE):
        unless = on_diagonal if d == 0 else None
        send(remote(hid_out, hid_in.at[r], 6, d, r, t, other(t, d)), unless)

    @pl.when(on_diagonal)
    def _():
        hid_in[r] = hid_out[...]

    text_keep[...] = text_part(t)
    loads[4].wait()
    for d in range(SIDE):
        q = other(r, d)
        receive(hid_in.at[q], 6, q, on_diagonal if d == 0 else None)

    merged = chunk_norm([hid_in[c].astype(jnp.float32) for c in range(SIDE)], merge_gain)
    before = f32_dot(merged[0], fc1_w[0:width])
    for c in range(1, SIDE):
        before = before + f32_dot(merged[c], fc1_w[c * width : (c + 1) * width])
    for q in range(SIDE):
        pre_own[q] = before[q * SLOTS : (q + 1) * SLOTS]
        pre_out[q] = before[q * SLOTS : (q + 1) * SLOTS].astype(jnp.bfloat16)
    for d in range(1, SIDE):
        p = other(r, d)
        send(remote(pre_out.at[p], pre_in.at[d - 1], 7, d, d, p, t))
    total = pre_own[r]
    for d in range(1, SIDE):
        receive(pre_in.at[d - 1], 7, d)
        total = total + pre_in[d - 1].astype(jnp.float32)
    act_out[...] = (0.5 * total * (1.0 + lax.erf(total * (0.5**0.5)))).astype(jnp.bfloat16)
    for d in range(1, SIDE):
        send(remote(act_out, act_in.at[r], 8, d, d, other(r, d), t))
    act_in[r] = act_out[...]
    table = image_table(counts, image_request, image_position, request_len, token_rows)
    slot_i = iota((SIDE * SLOTS, SIDE * SLOTS), 0)
    row_j = iota((SIDE * SLOTS, SIDE * SLOTS), 1)
    pick = jnp.zeros(slot_i.shape, jnp.float32)
    for source, _, run, owner, base in table:
        offset = row_j - source
        hit = (slot_i - (owner * SLOTS + base) == offset) & (offset >= 0) & (offset < run)
        pick = jnp.where(hit, 1.0, pick)
    pick = pick.astype(jnp.bfloat16)
    loads[5].wait()
    for d in range(1, SIDE):
        receive(act_in.at[other(r, SIDE - d)], 8, d)

    active = act_in[...].reshape(SIDE * SLOTS, act_in.shape[2])
    picked = f32_dot(pick, active).astype(jnp.bfloat16)
    outward = f32_dot(picked, fc2_w[...]).astype(jnp.bfloat16)
    for q in range(SIDE):
        vis_out[q] = outward[q * SLOTS : (q + 1) * SLOTS]
    for d in range(SIDE):
        q = other(r, d)
        unless = on_diagonal if d == 0 else None
        send(remote(vis_out.at[q], vis_in.at[t], 9, d, t, q, r), unless)

    @pl.when(on_diagonal)
    def _():
        vis_in[t] = vis_out[r]

    for d in range(SIDE):
        q = other(t, d)
        receive(vis_in.at[q], 9, q, on_diagonal if d == 0 else None)
    visual = vis_in[0].astype(jnp.float32)
    for q in range(1, SIDE):
        visual = visual + vis_in[q].astype(jnp.float32)
    visual = visual.astype(jnp.bfloat16).astype(jnp.float32)
    squares = jnp.sum(visual * visual, axis=1, keepdims=True)
    sq_out[...] = jnp.broadcast_to(squares, sq_out.shape)
    for d in range(1, SIDE):
        send(remote(sq_out, sq_in.at[d - 1], 10, d, d, r, other(t, d)))
    projected = f32_dot((visual * rms_gain[...]).astype(jnp.bfloat16), kv_w[...])
    row_out[...] = projected.astype(jnp.bfloat16)
    for d in range(1, SIDE):
        send(remote(row_out, row_in.at[d - 1], 11, d, d, r, other(t, d)))
    total = projected
    squares = sq_out[...]
    for d in range(1, SIDE):
        receive(sq_in.at[d - 1], 10, d)
        squares = squares + sq_in[d - 1]
        receive(row_in.at[d - 1], 11, d)
        total = total + row_in[d - 1].astype(jnp.float32)
    total = total * lax.rsqrt(squares[:, :1] / (SIDE * visual.shape[1]) + epsilon)
    place_i = iota((share, SLOTS), 0) + r * token_rows + t * share
    place_k = iota((share, SLOTS), 1)
    place = jnp.zeros((share, SLOTS), jnp.float32)
    for _, first, run, owner, base in table:
        offset = place_i - first
        hit = (owner == r) & (place_k - base == offset) & (offset >= 0) & (offset < run)
        place = jnp.where(hit, 1.0, place)
    placed = jnp.dot(
        place, total, preferred_element_type=jnp.float32, precision=lax.Precision.HIGHEST
    )
    taken = jnp.sum(place, axis=1, keepdims=True) > 0.5
    plain = text_keep[...]
    for k in (1, 2):
        receive(text_in.at[k], 13, k)
        plain = plain + text_in[k].astype(jnp.float32)
    stacked = jnp.where(taken, placed, plain)
    row_ids = iota((share, HEAD_DIM), 0) + r * token_rows + t * share
    live = row_ids < 0
    for k in range(lengths.shape[0]):
        inside = row_ids - k * request_len
        live = live | ((inside >= 0) & (inside < lengths[k]))
    heads = cache_ref.shape[1] // HEAD_DIM
    for h in range(heads):
        part = stacked[:, h * HEAD_DIM : (h + 1) * HEAD_DIM]
        if h < heads // 2:
            part = part * cosines[...] + pltpu.roll(part, HEAD_DIM // 2, 1) * sines[...]
        bound = limits[:, h * HEAD_DIM : (h + 1) * HEAD_DIM]
        part = jnp.where(live, jnp.clip(part, -bound, bound), 0.0)
        cache_ref[:, h * HEAD_DIM : (h + 1) * HEAD_DIM] = part.astype(jnp.bfloat16)
    for wait in pending:
        wait()


def cell_cache(
    request_len,
    token_rows,
    patch_counts,
    image_request,
    image_position,
    patches,
    vit_gain,
    merge_gain,
    rms_gain,
    qkv_weight,
    proj_weight,
    fc1_weight,
    fc2_weight,
    kv_flat,
    text_rows,
    request_lengths,
    kv_scale,
):
    rows, width = patches.shape
    hidden_w = fc1_weight.shape[1]
    share_w, kv_width = kv_flat.shape
    bf16, f32 = jnp.bfloat16, jnp.float32
    n = SIDE
    share = token_rows // n
    first_row = lax.axis_index("req") * token_rows + lax.axis_index("tp") * share
    positions = (first_row + jnp.arange(share, dtype=jnp.int32)) % request_len
    half_dim = HEAD_DIM // 2
    frequency = theta_base ** (-2.0 * jnp.arange(half_dim, dtype=jnp.float32) / HEAD_DIM)
    angles = positions.astype(jnp.float32)[:, None] * frequency[None, :]
    cosine = jnp.cos(angles)
    sine = jnp.sin(angles)
    smem = pl.BlockSpec(memory_space=pltpu.SMEM)
    vmem = pl.BlockSpec(memory_space=pltpu.VMEM)
    anywhere = pl.BlockSpec(memory_space=pl.ANY)
    buffers = [
        ((3, width, width), bf16),
        (proj_weight.shape, bf16),
        (fc1_weight.shape, bf16),
        (fc2_weight.shape, bf16),
        (kv_flat.shape, bf16),
        (text_rows.shape, bf16),
        None,
        ((n, rows, width), bf16),
        ((n, SLOTS, width), bf16),
        ((n, SLOTS, width), bf16),
        ((n, rows, width), bf16),
        ((n, rows, width), bf16),
        ((n, 3, rows, width), f32),
        ((n, 3, rows, width), bf16),
        ((n - 1, 3, rows, width), bf16),
        ((rows, width), bf16),
        ((n, rows, width), bf16),
        ((n, rows, width), f32),
        ((n - 1, rows, width), f32),
        ((rows, width), bf16),
        ((n, rows, width), bf16),
        ((n, SLOTS, hidden_w), f32),
        ((n, SLOTS, hidden_w), bf16),
        ((n - 1, SLOTS, hidden_w), bf16),
        ((SLOTS, hidden_w), bf16),
        ((n, SLOTS, hidden_w), bf16),
        ((n, SLOTS, share_w), bf16),
        ((n, SLOTS, share_w), bf16),
        ((SLOTS, kv_width), bf16),
        ((n - 1, SLOTS, kv_width), bf16),
        ((SLOTS, 128), f32),
        ((n - 1, SLOTS, 128), f32),
        ((n, 8, share), f32),
        ((n - 1, n, 8, share), f32),
        ((share, kv_width), f32),
        ((3, share, kv_width), bf16),
        ((3, share, kv_width), bf16),
        ((n, 8, share), f32),
    ]
    scratch = [
        pltpu.SemaphoreType.DMA((6,)) if b is None else pltpu.VMEM(*b) for b in buffers
    ] + [pltpu.SemaphoreType.DMA((14, n)), pltpu.SemaphoreType.DMA((14, n))]
    return pl.pallas_call(
        functools.partial(cell_kernel, request_len, token_rows),
        out_shape=jax.ShapeDtypeStruct((share, kv_width), bf16),
        in_specs=[smem] * 2 + [vmem] * 7 + [anywhere] * 6,
        out_specs=vmem,
        scratch_shapes=scratch,
        compiler_params=pltpu.CompilerParams(
            collective_id=0, has_side_effects=True, vmem_limit_bytes=48 * 1024 * 1024
        ),
        cost_estimate=pl.CostEstimate(
            flops=6 * 10**9, bytes_accessed=22 * 10**6, transcendentals=10**5
        ),
    )(
        jnp.stack([patch_counts, image_request, image_position]),
        request_lengths,
        patches,
        vit_gain.reshape(1, n * width),
        merge_gain.reshape(1, n * width),
        rms_gain.reshape(1, share_w),
        jnp.concatenate([cosine, cosine], axis=1),
        jnp.concatenate([-sine, sine], axis=1),
        jnp.repeat(clip_level * kv_scale.reshape(1, -1), QGROUP, axis=1),
        jnp.transpose(qkv_weight, (1, 0, 2)),
        proj_weight,
        fc1_weight,
        fc2_weight,
        kv_flat,
        text_rows,
    )


def square_body(
    patches,
    patch_counts,
    image_request,
    image_position,
    request_lengths,
    vit_gain,
    qkv_weight,
    proj_weight,
    merge_gain,
    fc1_weight,
    fc2_weight,
    text_rows,
    rms_gain,
    kv_weight,
    kv_scale,
):
    token_rows, share_w = text_rows.shape
    request_len = SIDE * token_rows // request_lengths.shape[0]
    share_rows = token_rows // SIDE
    kv_flat = kv_weight.reshape(share_w, -1)
    cache = cell_cache(
        request_len,
        token_rows,
        patch_counts,
        image_request,
        image_position,
        patches,
        vit_gain,
        merge_gain,
        rms_gain,
        qkv_weight,
        proj_weight,
        fc1_weight,
        fc2_weight,
        kv_flat,
        text_rows,
        request_lengths,
        kv_scale,
    )
    return cache.reshape(share_rows, 2, -1)


def solution(mesh):
    placed = (
        P(("groups", "req"), "tp"),
        P("groups", None),
        P("groups", None),
        P("groups", None),
        P("groups"),
        P(),
        P("req", None, "tp"),
        P("tp", "req"),
        P(),
        P("req", "tp"),
        P("tp", "req"),
        P(("groups", "req"), "tp"),
        P("tp"),
        P("tp", None, None),
        P(),
    )
    square = mesh.shape["req"] == SIDE and mesh.shape["tp"] == SIDE
    return jax.shard_map(
        square_body if square else general_body,
        mesh=mesh,
        in_specs=placed,
        out_specs=P(("groups", "req", "tp"), None, None),
        check_vma=False,
    )
```

```python
import functools

import jax
import jax.numpy as jnp
from jax import lax
from jax.experimental import pallas as pl
from jax.experimental.pallas import tpu as pltpu
from jax.sharding import PartitionSpec as P

VIT_HEADS = 16
VIT_HD = 80
D = 8192
KV_HEADS = 8
HEAD_DIM = 128
QGROUP = 64


epsilon = 1e-06
theta_base = 1000000.0
clip_level = 127.0


def layer_norm(values, gains):
    average = jnp.mean(values, axis=-1, keepdims=True)
    centred = values - average
    variance = jnp.mean(centred * centred, axis=-1, keepdims=True)
    return centred * lax.rsqrt(variance + epsilon) * gains


def patch_images(counts_row, patch_rows):
    bounds = jnp.cumsum(counts_row)
    row_ids = jnp.arange(patch_rows, dtype=jnp.int32)
    return jnp.sum((row_ids[:, None] >= bounds[None, :]).astype(jnp.int32), axis=1)


def attend(queries, keys_in, values_in, image_ids, factor):
    scores = (
        jnp.einsum("qhd,khd->hqk", queries, keys_in, preferred_element_type=jnp.float32) * factor
    )
    allowed = image_ids[:, None] == image_ids[None, :]
    scores = jnp.where(allowed[None], scores, -jnp.inf)
    weights = jax.nn.softmax(scores, axis=-1).astype(jnp.bfloat16)
    return jnp.einsum(
        "hqk,khd->qhd", weights, values_in, preferred_element_type=jnp.float32
    ).astype(jnp.bfloat16)


def visual_targets(patch_counts, image_request, image_position, merged_dev, request_len):
    merged_runs = patch_counts // 4
    run_ends = jnp.cumsum(merged_runs, axis=1)
    run_starts = run_ends - merged_runs
    row_ids = jnp.arange(merged_dev, dtype=jnp.int32)
    inside = (row_ids[None, :, None] >= run_starts[:, None, :]) & (
        row_ids[None, :, None] < run_ends[:, None, :]
    )
    offsets = image_request * request_len + image_position - run_starts
    target = jnp.sum(jnp.where(inside, offsets[:, None, :] + row_ids[None, :, None], 0), axis=2)
    is_live = jnp.any(inside, axis=2)
    return (target.reshape(-1), is_live.reshape(-1))


def rotate_keys(heads, positions):
    half_dim = heads.shape[-1] // 2
    frequency = theta_base ** (-2.0 * jnp.arange(half_dim, dtype=jnp.float32) / heads.shape[-1])
    angles = positions.astype(jnp.float32)[:, None] * frequency[None, :]
    cosine = jnp.cos(angles)[:, None, :]
    sine = jnp.sin(angles)[:, None, :]
    former = heads[..., :half_dim]
    latter = heads[..., half_dim:]
    return jnp.concatenate(
        [former * cosine - latter * sine, latter * cosine + former * sine], axis=-1
    )


def finish_cache(stacked, positions, live_rows, kv_scale):
    height = stacked.shape[0]
    rotated = rotate_keys(stacked[:, 0].reshape(height, KV_HEADS, HEAD_DIM), positions)
    joined = jnp.concatenate(
        [rotated.reshape(height, 1, KV_HEADS * HEAD_DIM), stacked[:, 1:2]], axis=1
    )
    bounds = jnp.repeat(clip_level * kv_scale, QGROUP, axis=1)
    clipped = jnp.clip(joined, -bounds, bounds)
    return jnp.where(live_rows[:, None, None], clipped, 0.0).astype(jnp.bfloat16)


def general_body(
    patches,
    patch_counts,
    image_request,
    image_position,
    request_lengths,
    vit_gain,
    qkv_weight,
    proj_weight,
    merge_gain,
    fc1_weight,
    fc2_weight,
    text_rows,
    rms_gain,
    kv_weight,
    kv_scale,
):
    req_devices = lax.axis_size("req")
    tp_devices = lax.axis_size("tp")
    req_index = lax.axis_index("req")
    tp_index = lax.axis_index("tp")
    patch_rows = patches.shape[0]
    merged_rows = patch_rows // 4
    token_rows = text_rows.shape[0]
    request_len = req_devices * token_rows // request_lengths.shape[0]
    local_heads = VIT_HEADS // tp_devices
    gathered = lax.all_gather(patches, "tp", axis=1, tiled=True)
    vit_width = gathered.shape[1]
    normed = layer_norm(gathered.astype(jnp.float32), vit_gain).astype(jnp.bfloat16)
    qkv_local = jnp.einsum(
        "pd,dcf->pcf",
        normed,
        lax.all_gather(qkv_weight, "req", axis=0, tiled=True),
        preferred_element_type=jnp.float32,
    ).astype(jnp.bfloat16)
    heads = qkv_local.reshape(patch_rows, 3, local_heads, VIT_HD)
    image_ids = patch_images(patch_counts[req_index], patch_rows)
    attended = attend(heads[:, 0], heads[:, 1], heads[:, 2], image_ids, VIT_HD ** (-0.5))
    flat_heads = attended.reshape(patch_rows, local_heads * VIT_HD)
    branch = jnp.dot(
        flat_heads,
        lax.all_gather(proj_weight, "req", axis=1, tiled=True),
        preferred_element_type=jnp.float32,
    )
    branch_total = lax.psum(branch, "tp")
    hidden = (gathered.astype(jnp.float32) + branch_total).astype(jnp.bfloat16)
    merged_norm = layer_norm(hidden.astype(jnp.float32), merge_gain).astype(jnp.bfloat16)
    merged = merged_norm.reshape(merged_rows, 4 * vit_width)
    feature_blocks = lax.all_to_all(merged, "req", split_axis=1, concat_axis=0, tiled=True)
    picked = feature_blocks
    before_gelu = lax.psum_scatter(
        jnp.dot(picked, fc1_weight, preferred_element_type=jnp.float32),
        "req",
        scatter_dimension=0,
        tiled=True,
    )
    activated = jax.nn.gelu(before_gelu, approximate=False).astype(jnp.bfloat16)
    outward = jnp.dot(
        lax.all_gather(activated, "req", axis=0, tiled=True),
        fc2_weight,
        preferred_element_type=jnp.float32,
    )
    target, is_live = visual_targets(
        patch_counts, image_request, image_position, merged_rows, request_len
    )
    all_rows = req_devices * token_rows
    slot_total = req_devices * merged_rows
    source_total = outward.shape[0]
    flags = (
        jnp.zeros((all_rows,), jnp.int32)
        .at[jnp.where(is_live, target, all_rows)]
        .set(1, mode="drop")
    )
    flag_grid = flags.reshape(req_devices, token_rows)
    ranks = (jnp.cumsum(flag_grid, axis=1) - flag_grid).reshape(-1)
    owners = target // token_rows
    slots = owners * merged_rows + ranks[jnp.clip(target, 0, all_rows - 1)]
    source_ids = jnp.arange(source_total, dtype=jnp.int32)
    picking = (
        jnp.full((slot_total,), source_total, jnp.int32)
        .at[jnp.where(is_live, slots, slot_total)]
        .set(source_ids, mode="drop")
    )
    padded = jnp.concatenate([outward, jnp.zeros((1, outward.shape[1]), jnp.float32)], axis=0)
    sending = padded[picking]
    arrived = lax.all_to_all(sending, "req", split_axis=0, concat_axis=1, tiled=True)
    visual = lax.psum_scatter(arrived, "tp", scatter_dimension=1, tiled=True).astype(jnp.bfloat16)
    local_flags = lax.dynamic_slice_in_dim(flags, req_index * token_rows, token_rows)
    local_ranks = lax.dynamic_slice_in_dim(ranks, req_index * token_rows, token_rows)
    chosen = visual[jnp.clip(local_ranks, 0, merged_rows - 1)]
    combined = jnp.where(local_flags[:, None] > 0, chosen, text_rows)
    wide_rows = combined.astype(jnp.float32)
    square_sums = lax.psum(jnp.sum(wide_rows * wide_rows, axis=1), "tp")
    scaled = (wide_rows * lax.rsqrt(square_sums[:, None] / D + epsilon) * rms_gain).astype(
        jnp.bfloat16
    )
    share_rows = token_rows // tp_devices
    picked = scaled
    stacked = lax.psum_scatter(
        jnp.einsum("rf,fcw->rcw", picked, kv_weight, preferred_element_type=jnp.float32),
        "tp",
        scatter_dimension=0,
        tiled=True,
    )
    row_ids = (
        req_index * token_rows + tp_index * share_rows + jnp.arange(share_rows, dtype=jnp.int32)
    )
    positions = row_ids % request_len
    live_rows = positions < request_lengths[row_ids // request_len]
    return finish_cache(stacked, positions, live_rows, kv_scale)


def iota(shape, dim):
    return lax.broadcasted_iota(jnp.int32, shape, dim)


def f32_dot(left, right):
    return jnp.dot(left, right, preferred_element_type=jnp.float32)


def image_table(counts, image_request, image_position, request_len, token_rows):
    images = []
    for s in range(counts.shape[0]):
        source = jnp.int32(s * SLOTS)
        for j in range(counts.shape[1]):
            run = counts[s, j] // 4
            first = image_request[s, j] * request_len + image_position[s, j]
            images.append((source, first, run, first // token_rows))
            source = source + run
    table = []
    for source, first, run, owner in images:
        base = jnp.int32(0)
        for _, other_first, other_run, other_owner in images:
            earlier = (other_owner == owner) & (other_first < first)
            base = base + jnp.where(earlier, other_run, 0)
        table.append((source, first, run, owner, base))
    return table


SLOTS = 16
SIDE = 4


def cell_kernel(
    request_len,
    token_rows,
    tables,
    lengths,
    patches,
    norm_gains,
    rms_gain,
    cosines,
    sines,
    limits,
    qkv_hbm,
    proj_hbm,
    fc1_hbm,
    fc2_hbm,
    kv_hbm,
    text_hbm,
    cache_ref,
    qkv_w,
    proj_w,
    fc1_w,
    fc2_w,
    kv_w,
    text_v,
    load_sem,
    patch_all,
    res_out,
    res_in,
    norm_out,
    norm_in,
    part_own,
    part_out,
    part_in,
    att_out,
    att_in,
    branch_own,
    branch_out,
    branch_in,
    hid_out,
    hid_in,
    pre_own,
    pre_out,
    pre_in,
    act_out,
    act_in,
    vis_out,
    vis_in,
    row_out,
    row_in,
    sq_out,
    sq_in,
    tsq_out,
    tsq_in,
    text_keep,
    text_out,
    text_in,
    sums,
    send_sem,
    recv_sem,
):
    r = lax.axis_index("req")
    t = lax.axis_index("tp")
    rows, width = patches.shape
    full = SIDE * width
    counts, image_request, image_position = (tables.at[k] for k in range(3))

    def other(i, d):
        return lax.rem(i + d, SIDE)

    loads = []
    for k, (src, dst) in enumerate(
        (
            (qkv_hbm, qkv_w),
            (text_hbm, text_v),
            (kv_hbm, kv_w),
            (proj_hbm, proj_w),
            (fc1_hbm, fc1_w),
            (fc2_hbm, fc2_w),
        )
    ):
        copy = pltpu.make_async_copy(src, dst, load_sem.at[k])
        copy.start()
        loads.append(copy)

    barrier = pltpu.get_barrier_semaphore()
    for a in range(SIDE):
        for b in range(SIDE):
            if a or b:
                pl.semaphore_signal(
                    barrier,
                    inc=1,
                    device_id={"req": other(r, a), "tp": other(t, b)},
                    device_id_type=pl.DeviceIdType.MESH,
                )
    pl.semaphore_wait(barrier, SIDE * SIDE - 1)

    pending = []

    def remote(src, dst, stage, s_index, r_index, to_r, to_t):
        return pltpu.make_async_remote_copy(
            src_ref=src,
            dst_ref=dst,
            send_sem=send_sem.at[stage, s_index],
            recv_sem=recv_sem.at[stage, r_index],
            device_id={"req": to_r, "tp": to_t},
            device_id_type=pl.DeviceIdType.MESH,
        )

    def send(copy, unless=None):
        if unless is None:
            copy.start()
            pending.append(copy.wait_send)
        else:
            pl.when(jnp.logical_not(unless))(copy.start)
            pending.append(lambda: pl.when(jnp.logical_not(unless))(copy.wait_send))

    def receive(dst, stage, index, unless=None):
        copy = remote(dst, dst, stage, 0, index, other(r, 1), t)
        if unless is None:
            copy.wait_recv()
        else:
            pl.when(jnp.logical_not(unless))(copy.wait_recv)

    on_diagonal = r == t

    for d in range(1, SIDE):
        send(remote(patches, patch_all.at[t], 0, d, d, r, other(t, d)))
    patch_all[t] = patches[...]
    picks_i = iota((rows, rows), 0)
    picks_j = iota((rows, rows), 1)
    by_class = jnp.where(
        picks_j == 4 * lax.rem(picks_i, SLOTS) + picks_i // SLOTS, 1.0, 0.0
    ).astype(jnp.bfloat16)
    regrouped = f32_dot(by_class, patches[...]).astype(jnp.bfloat16)
    for c in range(SIDE):
        res_out[c] = regrouped[c * SLOTS : (c + 1) * SLOTS]
    for d in range(SIDE):
        c = other(t, d)
        unless = on_diagonal if d == 0 else None
        send(remote(res_out.at[c], res_in.at[r], 1, d, r, t, c), unless)

    @pl.when(on_diagonal)
    def _():
        res_in[r] = res_out[t]

    share = cache_ref.shape[0]

    def text_chunk(c):
        return text_v[pl.ds(pl.multiple_of(c * share, share), share)].astype(jnp.float32)

    loads[1].wait()
    for c in range(SIDE):
        wide = text_chunk(c)
        column = jnp.sum(wide * wide, axis=1, keepdims=True)
        tsq_out[c] = jnp.transpose(jnp.broadcast_to(column, (share, share)))[:8]
    for d in range(1, SIDE):
        send(remote(tsq_out, tsq_in.at[d - 1], 12, d, d, r, other(t, d)))
    for d in range(1, SIDE):
        receive(patch_all.at[other(t, SIDE - d)], 0, d)

    def chunk_norm(values, k):
        total = jnp.sum(values[0], axis=1, keepdims=True)
        for v in values[1:]:
            total = total + jnp.sum(v, axis=1, keepdims=True)
        average = total / full
        centred = [v - average for v in values]
        total = jnp.sum(centred[0] * centred[0], axis=1, keepdims=True)
        for v in centred[1:]:
            total = total + jnp.sum(v * v, axis=1, keepdims=True)
        inverse = lax.rsqrt(total / full + epsilon)
        return [
            (v * inverse * norm_gains[k : k + 1, c * width : (c + 1) * width]).astype(jnp.bfloat16)
            for c, v in enumerate(centred)
        ]

    normed = chunk_norm([patch_all[c].astype(jnp.float32) for c in range(SIDE)], 0)
    for c in range(SIDE):
        norm_out[c] = normed[c]
    for d in range(1, SIDE):
        p = other(r, d)
        send(remote(norm_out.at[p], norm_in.at[r], 2, d, d, p, t))
    norm_in[r] = norm_out[r]
    for d in range(1, SIDE):
        receive(norm_in.at[other(r, SIDE - d)], 2, d)

    loads[0].wait()
    every = norm_in[...].reshape(SIDE * rows, width)
    for c in range(3):
        part = f32_dot(every, qkv_w[c]).reshape(SIDE, rows, width)
        part_own[:, c] = part
        part_out[:, c] = part.astype(jnp.bfloat16)
    for d in range(1, SIDE):
        p = other(r, d)
        send(remote(part_out.at[p], part_in.at[d - 1], 3, d, d, p, t))

    for d in range(1, SIDE):
        receive(tsq_in.at[d - 1], 12, d)
    for c in range(SIDE):
        tsq_out_sum = tsq_out[c]
        for d in range(1, SIDE):
            tsq_out_sum = tsq_out_sum + tsq_in[d - 1, c]
        sums[c] = tsq_out_sum
    loads[2].wait()
    mate = t + 1 - 2 * lax.rem(t, 2)
    across = other(t, 2)
    columns = text_v.shape[1]

    def text_part(c):
        squares = jnp.transpose(jnp.broadcast_to(sums[c][:1], (share, share)))[:, :1]
        inverse = lax.rsqrt(squares / (SIDE * columns) + epsilon)
        scaled = (text_chunk(c) * inverse * rms_gain[...]).astype(jnp.bfloat16)
        return f32_dot(scaled, kv_w[...])

    text_out[0] = text_part(other(mate, 2)).astype(jnp.bfloat16)
    send(remote(text_out.at[0], text_in.at[0], 13, 0, 0, r, mate))
    text_keep[...] = text_part(across)
    receive(text_in.at[0], 13, 0)
    text_out[1] = (text_keep[...] + text_in[0].astype(jnp.float32)).astype(jnp.bfloat16)
    send(remote(text_out.at[1], text_in.at[1], 13, 1, 1, r, across))

    total = part_own[r]
    for d in range(1, SIDE):
        receive(part_in.at[d - 1], 3, d)
        total = total + part_in[d - 1].astype(jnp.float32)
    qkv = total.astype(jnp.bfloat16)

    first_end = counts[r, 0]
    second_end = first_end + counts[r, 1]

    def ids(index):
        return (index >= first_end).astype(jnp.int32) + (index >= second_end).astype(jnp.int32)

    allowed = ids(picks_i) == ids(picks_j)
    lanes = iota((rows, width), 1) // VIT_HD
    attended = jnp.zeros((rows, width), jnp.float32)
    for h in range(width // VIT_HD):
        mine = lanes == h
        query = jnp.where(mine, qkv[0].astype(jnp.float32), 0.0).astype(jnp.bfloat16)
        value = jnp.where(mine, qkv[2].astype(jnp.float32), 0.0).astype(jnp.bfloat16)
        scores = lax.dot_general(
            query, qkv[1], (((1,), (1,)), ((), ())), preferred_element_type=jnp.float32
        ) * (VIT_HD ** (-0.5))
        scores = jnp.where(allowed, scores, -jnp.inf)
        weights = jnp.exp(scores - jnp.max(scores, axis=1, keepdims=True))
        weights = weights / jnp.sum(weights, axis=1, keepdims=True)
        attended = attended + f32_dot(weights.astype(jnp.bfloat16), value)
    att_out[...] = f32_dot(by_class, attended.astype(jnp.bfloat16)).astype(jnp.bfloat16)
    for d in range(1, SIDE):
        send(remote(att_out, att_in.at[r], 4, d, d, other(r, d), t))
    att_in[r] = att_out[...]
    text_out[2] = text_part(mate).astype(jnp.bfloat16)
    send(remote(text_out.at[2], text_in.at[2], 13, 2, 2, r, mate))
    loads[3].wait()
    for d in range(1, SIDE):
        receive(att_in.at[other(r, SIDE - d)], 4, d)

    branch = f32_dot(att_in[...].reshape(SIDE * rows, width), proj_w[...])
    branch = branch.reshape(SIDE, SIDE, SLOTS, width)
    for c in range(SIDE):
        branch_own[c] = branch[:, c].reshape(rows, width)
        branch_out[c] = branch_own[c].astype(jnp.bfloat16)
    for d in range(1, SIDE):
        c = other(t, d)
        send(remote(branch_out.at[c], branch_in.at[d - 1], 5, d, d, r, c))
    total = branch_own[t]
    for d in range(SIDE):
        q = other(r, d)
        receive(res_in.at[q], 1, q, on_diagonal if d == 0 else None)
    residual = res_in[...].reshape(rows, width).astype(jnp.float32)
    for d in range(1, SIDE):
        receive(branch_in.at[d - 1], 5, d)
        total = total + branch_in[d - 1].astype(jnp.float32)
    hid_out[...] = (residual + total).astype(jnp.bfloat16)
    for d in range(SIDE):
        unless = on_diagonal if d == 0 else None
        send(remote(hid_out, hid_in.at[r], 6, d, r, t, other(t, d)), unless)

    @pl.when(on_diagonal)
    def _():
        hid_in[r] = hid_out[...]

    text_keep[...] = text_part(t)
    loads[4].wait()
    for d in range(SIDE):
        q = other(r, d)
        receive(hid_in.at[q], 6, q, on_diagonal if d == 0 else None)

    merged = chunk_norm([hid_in[c].astype(jnp.float32) for c in range(SIDE)], 1)
    before = f32_dot(merged[0], fc1_w[0:width])
    for c in range(1, SIDE):
        before = before + f32_dot(merged[c], fc1_w[c * width : (c + 1) * width])
    for q in range(SIDE):
        pre_own[q] = before[q * SLOTS : (q + 1) * SLOTS]
        pre_out[q] = before[q * SLOTS : (q + 1) * SLOTS].astype(jnp.bfloat16)
    for d in range(1, SIDE):
        p = other(r, d)
        send(remote(pre_out.at[p], pre_in.at[d - 1], 7, d, d, p, t))
    total = pre_own[r]
    for d in range(1, SIDE):
        receive(pre_in.at[d - 1], 7, d)
        total = total + pre_in[d - 1].astype(jnp.float32)
    act_out[...] = (0.5 * total * (1.0 + lax.erf(total * (0.5**0.5)))).astype(jnp.bfloat16)
    for d in range(1, SIDE):
        send(remote(act_out, act_in.at[r], 8, d, d, other(r, d), t))
    act_in[r] = act_out[...]
    table = image_table(counts, image_request, image_position, request_len, token_rows)
    slot_i = iota((SIDE * SLOTS, SIDE * SLOTS), 0)
    row_j = iota((SIDE * SLOTS, SIDE * SLOTS), 1)
    pick = jnp.zeros(slot_i.shape, jnp.float32)
    for source, _, run, owner, base in table:
        offset = row_j - source
        hit = (slot_i - (owner * SLOTS + base) == offset) & (offset >= 0) & (offset < run)
        pick = jnp.where(hit, 1.0, pick)
    pick = pick.astype(jnp.bfloat16)
    loads[5].wait()
    for d in range(1, SIDE):
        receive(act_in.at[other(r, SIDE - d)], 8, d)

    active = act_in[...].reshape(SIDE * SLOTS, act_in.shape[2])
    picked = f32_dot(pick, active).astype(jnp.bfloat16)
    outward = f32_dot(picked, fc2_w[...]).astype(jnp.bfloat16)
    for q in range(SIDE):
        vis_out[q] = outward[q * SLOTS : (q + 1) * SLOTS]
    for d in range(SIDE):
        q = other(r, d)
        unless = on_diagonal if d == 0 else None
        send(remote(vis_out.at[q], vis_in.at[t], 9, d, t, q, r), unless)

    @pl.when(on_diagonal)
    def _():
        vis_in[t] = vis_out[r]

    for d in range(SIDE):
        q = other(t, d)
        receive(vis_in.at[q], 9, q, on_diagonal if d == 0 else None)
    visual = vis_in[0].astype(jnp.float32)
    for q in range(1, SIDE):
        visual = visual + vis_in[q].astype(jnp.float32)
    visual = visual.astype(jnp.bfloat16).astype(jnp.float32)
    squares = jnp.sum(visual * visual, axis=1, keepdims=True)
    sq_out[...] = jnp.broadcast_to(squares, sq_out.shape)
    for d in range(1, SIDE):
        send(remote(sq_out, sq_in.at[d - 1], 10, d, d, r, other(t, d)))
    projected = f32_dot((visual * rms_gain[...]).astype(jnp.bfloat16), kv_w[...])
    row_out[...] = projected.astype(jnp.bfloat16)
    for d in range(1, SIDE):
        send(remote(row_out, row_in.at[d - 1], 11, d, d, r, other(t, d)))
    total = projected
    squares = sq_out[...]
    for d in range(1, SIDE):
        receive(sq_in.at[d - 1], 10, d)
        squares = squares + sq_in[d - 1]
        receive(row_in.at[d - 1], 11, d)
        total = total + row_in[d - 1].astype(jnp.float32)
    total = total * lax.rsqrt(squares[:, :1] / (SIDE * visual.shape[1]) + epsilon)
    place_i = iota((share, SLOTS), 0) + r * token_rows + t * share
    place_k = iota((share, SLOTS), 1)
    place = jnp.zeros((share, SLOTS), jnp.float32)
    for _, first, run, owner, base in table:
        offset = place_i - first
        hit = (owner == r) & (place_k - base == offset) & (offset >= 0) & (offset < run)
        place = jnp.where(hit, 1.0, place)
    placed = jnp.dot(
        place, total, preferred_element_type=jnp.float32, precision=lax.Precision.HIGHEST
    )
    taken = jnp.sum(place, axis=1, keepdims=True) > 0.5
    plain = text_keep[...]
    for k in (1, 2):
        receive(text_in.at[k], 13, k)
        plain = plain + text_in[k].astype(jnp.float32)
    stacked = jnp.where(taken, placed, plain)
    row_ids = iota((share, HEAD_DIM), 0) + r * token_rows + t * share
    live = row_ids < 0
    for k in range(lengths.shape[0]):
        inside = row_ids - k * request_len
        live = live | ((inside >= 0) & (inside < lengths[k]))
    heads = cache_ref.shape[1] // HEAD_DIM
    for h in range(heads):
        part = stacked[:, h * HEAD_DIM : (h + 1) * HEAD_DIM]
        if h < heads // 2:
            part = part * cosines[...] + pltpu.roll(part, HEAD_DIM // 2, 1) * sines[...]
        bound = limits[:, h * HEAD_DIM : (h + 1) * HEAD_DIM]
        part = jnp.where(live, jnp.clip(part, -bound, bound), 0.0)
        cache_ref[:, h * HEAD_DIM : (h + 1) * HEAD_DIM] = part.astype(jnp.bfloat16)
    for wait in pending:
        wait()


def cell_cache(
    request_len,
    token_rows,
    patch_counts,
    image_request,
    image_position,
    patches,
    vit_gain,
    merge_gain,
    rms_gain,
    qkv_weight,
    proj_weight,
    fc1_weight,
    fc2_weight,
    kv_flat,
    text_rows,
    request_lengths,
    kv_scale,
):
    rows, width = patches.shape
    hidden_w = fc1_weight.shape[1]
    share_w, kv_width = kv_flat.shape
    bf16, f32 = jnp.bfloat16, jnp.float32
    n = SIDE
    share = token_rows // n
    first_row = lax.axis_index("req") * token_rows + lax.axis_index("tp") * share
    positions = (first_row + jnp.arange(share, dtype=jnp.int32)) % request_len
    half_dim = HEAD_DIM // 2
    frequency = theta_base ** (-2.0 * jnp.arange(half_dim, dtype=jnp.float32) / HEAD_DIM)
    angles = positions.astype(jnp.float32)[:, None] * frequency[None, :]
    cosine = jnp.cos(angles)
    sine = jnp.sin(angles)
    smem = pl.BlockSpec(memory_space=pltpu.SMEM)
    vmem = pl.BlockSpec(memory_space=pltpu.VMEM)
    anywhere = pl.BlockSpec(memory_space=pl.ANY)
    buffers = [
        ((3, width, width), bf16),
        (proj_weight.shape, bf16),
        (fc1_weight.shape, bf16),
        (fc2_weight.shape, bf16),
        (kv_flat.shape, bf16),
        (text_rows.shape, bf16),
        None,
        ((n, rows, width), bf16),
        ((n, SLOTS, width), bf16),
        ((n, SLOTS, width), bf16),
        ((n, rows, width), bf16),
        ((n, rows, width), bf16),
        ((n, 3, rows, width), f32),
        ((n, 3, rows, width), bf16),
        ((n - 1, 3, rows, width), bf16),
        ((rows, width), bf16),
        ((n, rows, width), bf16),
        ((n, rows, width), f32),
        ((n, rows, width), bf16),
        ((n - 1, rows, width), bf16),
        ((rows, width), bf16),
        ((n, rows, width), bf16),
        ((n, SLOTS, hidden_w), f32),
        ((n, SLOTS, hidden_w), bf16),
        ((n - 1, SLOTS, hidden_w), bf16),
        ((SLOTS, hidden_w), bf16),
        ((n, SLOTS, hidden_w), bf16),
        ((n, SLOTS, share_w), bf16),
        ((n, SLOTS, share_w), bf16),
        ((SLOTS, kv_width), bf16),
        ((n - 1, SLOTS, kv_width), bf16),
        ((SLOTS, 128), f32),
        ((n - 1, SLOTS, 128), f32),
        ((n, 8, share), f32),
        ((n - 1, n, 8, share), f32),
        ((share, kv_width), f32),
        ((3, share, kv_width), bf16),
        ((3, share, kv_width), bf16),
        ((n, 8, share), f32),
    ]
    scratch = [
        pltpu.SemaphoreType.DMA((6,)) if b is None else pltpu.VMEM(*b) for b in buffers
    ] + [pltpu.SemaphoreType.DMA((14, n)), pltpu.SemaphoreType.DMA((14, n))]
    return pl.pallas_call(
        functools.partial(cell_kernel, request_len, token_rows),
        out_shape=jax.ShapeDtypeStruct((share, kv_width), bf16),
        in_specs=[smem] * 2 + [vmem] * 6 + [anywhere] * 6,
        out_specs=vmem,
        scratch_shapes=scratch,
        compiler_params=pltpu.CompilerParams(
            collective_id=0, has_side_effects=True, vmem_limit_bytes=48 * 1024 * 1024
        ),
        cost_estimate=pl.CostEstimate(
            flops=6 * 10**9, bytes_accessed=22 * 10**6, transcendentals=10**5
        ),
    )(
        jnp.stack([patch_counts, image_request, image_position]),
        request_lengths,
        patches,
        jnp.stack([vit_gain, merge_gain]),
        rms_gain.reshape(1, share_w),
        jnp.concatenate([cosine, cosine], axis=1),
        jnp.concatenate([-sine, sine], axis=1),
        jnp.repeat(clip_level * kv_scale.reshape(1, -1), QGROUP, axis=1),
        jnp.transpose(qkv_weight, (1, 0, 2)),
        proj_weight,
        fc1_weight,
        fc2_weight,
        kv_flat,
        text_rows,
    )


def square_body(
    patches,
    patch_counts,
    image_request,
    image_position,
    request_lengths,
    vit_gain,
    qkv_weight,
    proj_weight,
    merge_gain,
    fc1_weight,
    fc2_weight,
    text_rows,
    rms_gain,
    kv_weight,
    kv_scale,
):
    token_rows, share_w = text_rows.shape
    request_len = SIDE * token_rows // request_lengths.shape[0]
    share_rows = token_rows // SIDE
    kv_flat = kv_weight.reshape(share_w, -1)
    cache = cell_cache(
        request_len,
        token_rows,
        patch_counts,
        image_request,
        image_position,
        patches,
        vit_gain,
        merge_gain,
        rms_gain,
        qkv_weight,
        proj_weight,
        fc1_weight,
        fc2_weight,
        kv_flat,
        text_rows,
        request_lengths,
        kv_scale,
    )
    return cache.reshape(share_rows, 2, -1)


def solution(mesh):
    placed = (
        P(("groups", "req"), "tp"),
        P("groups", None),
        P("groups", None),
        P("groups", None),
        P("groups"),
        P(),
        P("req", None, "tp"),
        P("tp", "req"),
        P(),
        P("req", "tp"),
        P("tp", "req"),
        P(("groups", "req"), "tp"),
        P("tp"),
        P("tp", None, None),
        P(),
    )
    square = mesh.shape["req"] == SIDE and mesh.shape["tp"] == SIDE
    return jax.shard_map(
        square_body if square else general_body,
        mesh=mesh,
        in_specs=placed,
        out_specs=P(("groups", "req", "tp"), None, None),
        check_vma=False,
    )
```
